256 devices in a mesh: section: 8 (over z_lo, core), dom: 32 (over y, z_hi, x).
Axes of the slice: x: 4, y: 4, z: 8 (z_hi: 2, z_lo: 4; z = z_hi * 4 + z_lo), core: 2. Of those that a mesh axis runs over, the one named last changes fastest.
Arguments:
- blocks: float32 [64, 64, 6, 128, 128], P('section', 'dom'), may hold values from -0.21875 to 0.21875
- column_index: int32 [64, 64, 6], P('section', 'dom'), may hold values from 0 to 63
- block_period: int32 [64, 64, 6], P('section', 'dom'), may hold values from 0 to 63, as said below
- cost_vector: float32 [64, 8192], P('section', 'dom'), may hold values from -6 to 6
- demand: float32 [64, 8192], P('section', 'dom'), may hold values from -12 to 12
- primal_start: float32 [64, 8192], P('section', 'dom'), may hold values from 0 to 2
- dual_start: float32 [64, 8192], P('section', 'dom'), may hold values from -3 to 3
- primal_weight: float32 [1], replicated, may hold values from 0.5 to 2
Outputs:
- primal_final: float32 [64, 8192], P('section', 'dom')
- dual_final: float32 [64, 8192], P('section', 'dom')
The draws below stay inside these ranges and needn't reach their ends.
Inputs may be any that keep to these rules, and one draw needn't show every extreme that they name: block_period[p, r, k] is p or p - 1; it is p for k = 0 and for p = 0.
All inputs are finite; a program needn't handle non-finite values.
Results may differ from the reference program's by a relative error of at most 0.00011.
Values sent between devices are 32-bit elements; how exact they have to be, the bound alone decides.
No kernel may reach another device: no remote copies, remote signals or barrier semaphores. Data moves between devices by JAX's collectives and lax.ppermute only.
A program may use at most 64 MiB of HBM per device.

```python
import math
import jax
import jax.numpy as jnp
from jax import lax

B = 128
NNZB = 6
PERIODS = 64
NBP = 64


def draw_block_period(key, part):
    own_period = jnp.arange(PERIODS, dtype=jnp.int32)[:, None, None]
    stepped = jax.random.randint(key, (PERIODS, NBP, NNZB), 0, 2).astype(jnp.int32)
    later_slot = (jnp.arange(NNZB, dtype=jnp.int32) > 0).astype(jnp.int32)[None, None, :]
    later_period = (own_period > 0).astype(jnp.int32)
    return (own_period - stepped * later_slot * later_period).astype(jnp.int32)


def draw_demand(key, part):
    rising = 1.0 + 2.0 * jnp.arange(PERIODS, dtype=jnp.float32)[:, None] / max(PERIODS - 1, 1)
    base_values = jax.random.truncated_normal(key, -4.0, 4.0, (PERIODS, NBP * B), jnp.float32)
    values = base_values * rising
    return values.astype(jnp.float32)


def with_ends(result, own_key, low, largest):
    extent = result.shape
    place = [jax.random.randint(jax.random.fold_in(own_key, axis), (), 0, extent[axis]) for axis in range(len(extent))]
    result = result.at[tuple(place)].set(low)
    longest = extent.index(max(extent))
    place[longest] = (place[longest] + 1) % extent[longest]
    return result.at[tuple(place)].set(largest)


def levels(rng, shape, pieces, smallest, largest):
    gain, own = 1.0, jax.random.fold_in(rng, 6)
    for dim, blocks in pieces:
        heights = jnp.exp(jax.random.uniform(jax.random.fold_in(own, dim), (blocks,), jnp.float32, smallest / len(pieces), largest / len(pieces)))
        gain = gain * jnp.repeat(heights, shape[dim] // blocks).reshape([-1 if axis == dim else 1 for axis in range(len(shape))])
    return gain


def scatter_about(stream_key, dims, width, limit, cuts=(), kind=jnp.bfloat16):
    result = jax.random.normal(stream_key, dims, jnp.float32) * width
    if len(cuts) > 0:
        result = levels(stream_key, dims, cuts, -0.22, 0.18) * result
    return jnp.clip(result, min=-limit, max=limit).astype(kind)


def setup_inputs(seed: int = 0) -> dict:
    seeds = jax.random.split(jax.random.key(seed), 9)
    return {
        "blocks": scatter_about(seeds[0], (PERIODS, NBP, NNZB, B, B), (NNZB * B) ** -0.5, 0.21875, ((0, 8), (1, 32)), jnp.float32),
        "column_index": with_ends(jax.random.randint(seeds[1], (PERIODS, NBP, NNZB), 0, NBP), jax.random.fold_in(seeds[1], 1), 0, NBP - 1).astype(jnp.int32),
        "block_period": draw_block_period(jax.random.fold_in(seeds[8], 71), 0),
        "cost_vector": scatter_about(seeds[3], (PERIODS, NBP * B), 1.0, 6.0, ((0, 8), (1, 32)), jnp.float32),
        "demand": draw_demand(jax.random.fold_in(seeds[8], 71), 0),
        "primal_start": jnp.clip(2.0 * jax.random.uniform(seeds[5], (PERIODS, NBP * B), jnp.float32) ** levels(seeds[5], (PERIODS, NBP * B), ((0, 8), (1, 32)), -0.2, 0.2), 0.0, 2.0),
        "dual_start": scatter_about(seeds[6], (PERIODS, NBP * B), 0.5, 3.0, ((0, 8), (1, 32)), jnp.float32),
        "primal_weight": jnp.clip(jnp.exp(jax.random.uniform(seeds[7], (1,), jnp.float32, math.log(0.5), math.log(2.0))), 0.5, 2.0),
    }


step_scale = 0.4
epsilon = 1e-06

def forward(blocks, column_index, block_period, field):
    field_blocks = field.reshape(PERIODS, NBP, B)
    picked = field_blocks[block_period, column_index]
    product = jnp.einsum('prkij,prkj->pri', blocks, picked, precision=lax.Precision.HIGHEST)
    return product.reshape(PERIODS, NBP * B)

def adjoint(blocks, column_index, block_period, field):
    field_blocks = field.reshape(PERIODS, NBP, B)
    block_terms = jnp.einsum('prkij,pri->prkj', blocks, field_blocks, precision=lax.Precision.HIGHEST)
    segment_ids = (block_period * NBP + column_index).reshape(-1).astype(jnp.int32)
    summed = jax.ops.segment_sum(block_terms.reshape(-1, B), segment_ids, num_segments=PERIODS * NBP)
    return summed.reshape(PERIODS, NBP * B)

def reference(blocks, column_index, block_period, cost_vector, demand, primal_start, dual_start, primal_weight):
    weight_now = primal_weight[0]
    tau_first = step_scale / weight_now
    sigma_first = step_scale * weight_now
    primal_one = jnp.maximum(0.0, primal_start - tau_first * (cost_vector - adjoint(blocks, column_index, block_period, dual_start)))
    dual_one = dual_start + sigma_first * (demand - forward(blocks, column_index, block_period, 2.0 * primal_one - primal_start))
    move_primal = jnp.sum((primal_one - primal_start) ** 2)
    move_dual = jnp.sum((dual_one - dual_start) ** 2)
    weight_next = jnp.sqrt(weight_now * jnp.sqrt((move_dual + epsilon) / (move_primal + epsilon)))
    tau_second = step_scale / weight_next
    sigma_second = step_scale * weight_next
    primal_final = jnp.maximum(0.0, primal_one - tau_second * (cost_vector - adjoint(blocks, column_index, block_period, dual_one)))
    dual_final = dual_one + sigma_second * (demand - forward(blocks, column_index, block_period, 2.0 * primal_final - primal_one))
    return (primal_final, dual_final)
```

```python
import functools

import jax
import jax.numpy as jnp
from jax import lax
from jax.experimental import pallas as pl
from jax.experimental.pallas import tpu as pltpu
from jax.sharding import Mesh
from jax.sharding import PartitionSpec as P

AXES = ("section_0", "section_1", "dom_0", "dom_1", "dom_2")
SECTION = ("section_0", "section_1")
DOM = ("dom_0", "dom_1", "dom_2")
PLANE = ("dom_0", "dom_2")
TWIN = "dom_1"

step_scale = 0.4
epsilon = 1e-06

PEERS = 16
PERIODS_HERE = 8
LATER = tuple(range(1, 8))
CHUNK = 32
PIECE = 40

f32 = jnp.float32
VMEM = pl.BlockSpec(memory_space=pltpu.VMEM)
SMEM = pl.BlockSpec(memory_space=pltpu.SMEM)
PARAMS = pltpu.CompilerParams(vmem_limit_bytes=32 << 20)


def shaped(*shape):
    return jax.ShapeDtypeStruct(shape, f32)


def call(kernel, outs, ins, scratch=(), alias={}):
    return pl.pallas_call(
        kernel,
        out_shape=outs,
        in_specs=ins,
        out_specs=jax.tree.map(lambda _: VMEM, outs),
        scratch_shapes=list(scratch),
        input_output_aliases=alias,
        compiler_params=PARAMS,
    )


def columns_of(ref):
    rows = jnp.concatenate([ref[:, :128], ref[:, 128:], jnp.zeros((112, 128), f32)], axis=0)
    return rows.T


def store_rows(ref, rows):
    ref[:, :128] = rows[0:8]
    ref[:, 128:] = rows[8:16]


def transposed_product(block, wide):
    return jnp.sum(block * wide, axis=0, keepdims=True)


def partial_row(row):
    return row + (row >> 5) * 8


def slot(t, r, k):
    return t * 12 + r * 6 + k


def add_terms(blocks_ref, index_ref, dest_ref, t, r, wide, spread):
    for k in range(6):
        row = index_ref[slot(t, r, k)]
        if spread:
            row = partial_row(row)
        dest_ref[pl.ds(row, 1), :] += transposed_product(blocks_ref[t, r, k], wide)


def row_product(blocks_ref, index_ref, source_ref, t, r):
    total = jnp.zeros((128, 128), f32)
    for k in range(6):
        total += blocks_ref[t, r, k] * source_ref[pl.ds(index_ref[slot(t, r, k)], 1), :]
    return jnp.sum(total, axis=1, keepdims=True)


def adjoint_first(index_ref, blocks_ref, dual_ref, own_ref, carry_ref, terms):
    terms[...] = jnp.zeros_like(terms)
    columns = columns_of(dual_ref)
    for r in range(2):
        wide = jnp.broadcast_to(columns[:, r * 8 : r * 8 + 1], (128, 128))
        add_terms(blocks_ref, index_ref, terms, 0, r, wide, False)
    own_ref[...] = terms[0:64]
    carry_ref[...] = terms[64:128]


def adjoint_later(index_ref, blocks_ref, dual_ref, own_ref, partial_ref):
    partial_ref[...] = jnp.zeros_like(partial_ref)
    for p in range(PEERS):
        partial_ref[pl.ds(p * PIECE, 4, stride=8), :] = own_ref[p * 4 : p * 4 + 4]
    columns = columns_of(dual_ref)
    for t in LATER:
        for r in range(2):
            place = r * 8 + t
            wide = jnp.broadcast_to(columns[:, place : place + 1], (128, 128))
            add_terms(blocks_ref, index_ref, partial_ref, t, r, wide, True)


def add_carried(partial_in, carried_ref, partial_ref):
    for p in range(PEERS):
        rows = pl.ds(p * PIECE + 7, 4, stride=8)
        partial_ref[rows, :] = partial_in[rows, :] + carried_ref[p * 4 : p * 4 + 4]


def add_own_and_carried(partial_in, own_ref, carried_ref, move_x, move_a, move_b, partial_ref):
    for p in range(PEERS):
        rows = pl.ds(p * PIECE, 4, stride=8)
        partial_ref[rows, :] = partial_in[rows, :] + own_ref[p * 4 : p * 4 + 4]
        rows = pl.ds(p * PIECE + 7, 4, stride=8)
        partial_ref[rows, :] = partial_in[rows, :] + carried_ref[p * 4 : p * 4 + 4]
    tile = jnp.concatenate([move_x[...], move_a[...] + move_b[...], jnp.zeros((6, 128), f32)], 0)
    for p in range(PEERS):
        partial_ref[p * PIECE + CHUNK : (p + 1) * PIECE, :] = tile


def total_of(pieces_ref):
    total = pieces_ref[0]
    for p in range(1, PEERS):
        total = total + pieces_ref[p]
    return total


def sum_and_pack(pieces_ref, primal_ref, cost_ref, pack_ref):
    pack_ref[0:CHUNK, :] = total_of(pieces_ref)[0:CHUNK]
    pack_ref[32:40, :] = primal_ref[:, :128]
    pack_ref[40:48, :] = primal_ref[:, 128:]
    pack_ref[48:56, :] = cost_ref[:, :128]
    pack_ref[56:64, :] = cost_ref[:, 128:]


def sum_only(pieces_ref, sum_ref):
    sum_ref[...] = total_of(pieces_ref)


def both_twins(own, other):
    first = lax.axis_index(TWIN) == 0
    return jnp.concatenate(
        [jnp.where(first, own, other), jnp.where(first, other, own)], axis=0
    )


def to_all(ref, value):
    for p in range(PEERS):
        ref[p] = value


def primal_step(weight_ref, pack_ref, other_ref, copies_ref, primal_one_ref, cost_ref, move_ref):
    tau = step_scale / jnp.full((CHUNK, 128), weight_ref[0], f32)
    product = pack_ref[0:32] + other_ref[0:32]
    start = both_twins(pack_ref[32:48], other_ref[32:48])
    cost = both_twins(pack_ref[48:64], other_ref[48:64])
    primal_one = jnp.maximum(0.0, start - tau * (cost - product))
    primal_one_ref[...] = primal_one
    cost_ref[...] = cost
    move_ref[...] = 0.5 * jnp.sum((primal_one - start) ** 2, axis=0, keepdims=True)
    to_all(copies_ref, 2.0 * primal_one - start)


def dual_later(
    index_ref, weight_ref, blocks_ref, field_ref, dual_ref, demand_ref, dual_one_ref, partial_ref, move_ref
):
    partial_ref[...] = jnp.zeros_like(partial_ref)
    sigma = step_scale * weight_ref[0]
    start = columns_of(dual_ref)
    demand = columns_of(demand_ref)
    lane = lax.broadcasted_iota(jnp.int32, (128, 128), 1)
    result = start
    for t in LATER:
        for r in range(2):
            place = r * 8 + t
            here = slice(place, place + 1)
            product = row_product(blocks_ref, index_ref, field_ref, t, r)
            dual_one = start[:, here] + sigma * (demand[:, here] - product)
            wide = jnp.broadcast_to(dual_one, (128, 128))
            result = jnp.where(lane == place, wide, result)
            add_terms(blocks_ref, index_ref, partial_ref, t, r, wide, True)
    move_ref[...] = jnp.sum((result - start).T ** 2, axis=0, keepdims=True)
    store_rows(dual_one_ref, result.T)


def first_rows(field_ref, carried_ref, rows):
    rows[0:64, :] = field_ref[pl.ds(0, 64, stride=8), :]
    rows[64:128, :] = carried_ref[...]


def dual_first(
    index_ref, weight_ref, blocks_ref, field_ref, carried_ref, dual_ref, demand_ref, later_ref,
    dual_one_ref, own_ref, carry_ref, move_ref, rows, terms,
):
    first_rows(field_ref, carried_ref, rows)
    terms[...] = jnp.zeros_like(terms)
    sigma = step_scale * weight_ref[0]
    start = columns_of(dual_ref)
    demand = columns_of(demand_ref)
    later = columns_of(later_ref)
    lane = lax.broadcasted_iota(jnp.int32, (128, 128), 1)
    result = start
    for r in range(2):
        here = slice(r * 8, r * 8 + 1)
        product = row_product(blocks_ref, index_ref, rows, 0, r)
        dual_one = start[:, here] + sigma * (demand[:, here] - product)
        wide = jnp.broadcast_to(dual_one, (128, 128))
        result = jnp.where(lane == r * 8, wide, result)
        later = jnp.where(lane == r * 8, wide, later)
        add_terms(blocks_ref, index_ref, terms, 0, r, wide, False)
    move_ref[...] = jnp.sum((result - start).T ** 2, axis=0, keepdims=True)
    store_rows(dual_one_ref, later.T)
    own_ref[...] = terms[0:64]
    carry_ref[...] = terms[64:128]


def spread_moves(sum_ref, other_ref, copies_ref):
    tile = sum_ref[CHUNK:PIECE] + other_ref[CHUNK:PIECE]
    for s in range(8):
        copies_ref[s] = tile


def primal_last(
    weight_ref, moves_ref, sum_ref, other_ref, primal_one_ref, cost_ref, copies_ref, primal_ref, steps_ref
):
    tile = moves_ref[0]
    for s in range(1, 8):
        tile = tile + moves_ref[s]
    move = jnp.broadcast_to(jnp.sum(tile, axis=1, keepdims=True), (8, 128))
    move_primal, move_dual = move[0:1], move[1:2]
    weight = jnp.full((1, 128), weight_ref[0], f32)
    omega = jnp.sqrt(weight * jnp.sqrt((move_dual + epsilon) / (move_primal + epsilon)))
    tau = step_scale / omega
    steps_ref[...] = jnp.broadcast_to(step_scale * omega, (8, 128))
    product = sum_ref[0:CHUNK] + other_ref[0:CHUNK]
    primal_one = primal_one_ref[...]
    primal = jnp.maximum(0.0, primal_one - tau * (cost_ref[...] - product))
    to_all(copies_ref, 2.0 * primal - primal_one)
    first = lax.axis_index(TWIN) == 0
    primal_ref[:, :128] = jnp.where(first, primal[0:8], primal[16:24])
    primal_ref[:, 128:] = jnp.where(first, primal[8:16], primal[24:32])


def last_later(index_ref, blocks_ref, field_ref, product_ref):
    lane = lax.broadcasted_iota(jnp.int32, (128, 128), 1)
    result = jnp.zeros((128, 128), f32)
    for t in LATER:
        for r in range(2):
            product = row_product(blocks_ref, index_ref, field_ref, t, r)
            result = jnp.where(lane == r * 8 + t, jnp.broadcast_to(product, (128, 128)), result)
    product_ref[...] = result


def last_first(
    index_ref, blocks_ref, field_ref, carried_ref, steps_ref, product_ref, dual_ref, demand_ref, out_ref, rows
):
    first_rows(field_ref, carried_ref, rows)
    lane = lax.broadcasted_iota(jnp.int32, (128, 128), 1)
    result = product_ref[...]
    for r in range(2):
        product = row_product(blocks_ref, index_ref, rows, 0, r)
        result = jnp.where(lane == r * 8, jnp.broadcast_to(product, (128, 128)), result)
    result = result.T
    sigma = steps_ref[...]
    for r in range(2):
        part = slice(r * 128, r * 128 + 128)
        out_ref[:, part] = dual_ref[:, part] + sigma * (
            demand_ref[:, part] - result[r * 8 : r * 8 + 8]
        )


def to_next(x, distance):
    route = [(i - distance, i) for i in range(8) if 0 <= i - distance < 8]
    return lax.ppermute(x, SECTION, route)


def to_twin(x):
    return lax.ppermute(x, TWIN, [(0, 1), (1, 0)])


def exchange(pieces, axis):
    return lax.all_to_all(pieces, axis, split_axis=0, concat_axis=0, tiled=True)


def block_rows(column_index, block_period):
    t = lax.broadcasted_iota(jnp.int32, column_index.shape, 0)
    period = lax.axis_index(SECTION) * PERIODS_HERE + t
    before = period - block_period
    c = column_index
    place = ((c >> 4) * 4 + ((c >> 1) & 3)) * 4 + ((c >> 3) & 1) * 2 + (c & 1)
    row = jnp.where(t == 0, place + 64 * before, place * 8 + t - before)
    return row.reshape(-1)


def on_device(
    blocks, column_index, block_period, cost_vector, demand, primal_start, dual_start, primal_weight
):
    index = block_rows(column_index, block_period)
    terms = pltpu.VMEM((128, 128), f32)
    half = shaped(64, 128)
    line = shaped(1, 128)
    partials = shaped(PEERS * PIECE, 128)
    chunk = shaped(CHUNK, 128)
    copies = shaped(PEERS, CHUNK, 128)
    local = shaped(8, 256)

    own, carry = call(adjoint_first, [half, half], [SMEM, VMEM, VMEM], [terms])(
        index, blocks, dual_start
    )
    carried = to_next(carry, -1)
    partial = call(adjoint_later, partials, [SMEM, VMEM, VMEM, VMEM])(index, blocks, dual_start, own)
    partial = call(add_carried, partials, [VMEM, VMEM], alias={0: 0})(partial, carried)
    pieces = exchange(partial.reshape(PEERS, PIECE, 128), PLANE)
    pack = call(sum_and_pack, shaped(64, 128), [VMEM] * 3)(pieces, primal_start, cost_vector)
    other = to_twin(pack)
    send, primal_one, cost, move_primal = call(
        primal_step, [copies, chunk, chunk, line], [SMEM, VMEM, VMEM]
    )(primal_weight, pack, other)
    field = exchange(send, PLANE).reshape(PEERS * CHUNK, 128)
    carried = to_next(field.reshape(64, 8, 128)[:, 7], 1)
    dual_some, partial, move_a = call(
        dual_later, [local, partials, line], [SMEM, SMEM] + [VMEM] * 4
    )(index, primal_weight, blocks, field, dual_start, demand)
    dual_one, own, carry, move_b = call(
        dual_first, [local, half, half, line], [SMEM, SMEM] + [VMEM] * 6, [terms, terms]
    )(index, primal_weight, blocks, field, carried, dual_start, demand, dual_some)
    carried = to_next(carry, -1)
    partial = call(add_own_and_carried, partials, [VMEM] * 6, alias={0: 0})(
        partial, own, carried, move_primal, move_a, move_b
    )
    pieces = exchange(partial.reshape(PEERS, PIECE, 128), PLANE)
    total = call(sum_only, shaped(PIECE, 128), [VMEM])(pieces)
    other = to_twin(total)
    moves = call(spread_moves, shaped(8, 8, 128), [VMEM] * 2)(total, other)
    moves = exchange(moves, SECTION)
    send, primal_final, steps = call(
        primal_last, [copies, local, shaped(8, 128)], [SMEM] + [VMEM] * 5
    )(primal_weight, moves, total, other, primal_one, cost)
    field = exchange(send, PLANE).reshape(PEERS * CHUNK, 128)
    carried = to_next(field.reshape(64, 8, 128)[:, 7], 1)
    product = call(last_later, shaped(128, 128), [SMEM, VMEM, VMEM])(index, blocks, field)
    dual_final = call(last_first, local, [SMEM] + [VMEM] * 7, [terms])(
        index, blocks, field, carried, steps, product, dual_one, demand
    )
    return primal_final, dual_final


def solution(mesh):
    finer = Mesh(mesh.devices.reshape(4, 2, 4, 2, 4), AXES)
    return jax.shard_map(
        on_device,
        mesh=finer,
        in_specs=(
            P(SECTION, DOM, None, None, None),
            P(SECTION, DOM, None),
            P(SECTION, DOM, None),
            P(SECTION, DOM),
            P(SECTION, DOM),
            P(SECTION, DOM),
            P(SECTION, DOM),
            P(),
        ),
        out_specs=(P(SECTION, DOM), P(SECTION, DOM)),
        check_vma=False,
    )
```

```python
import functools

import jax
import jax.numpy as jnp
from jax import lax
from jax.experimental import pallas as pl
from jax.experimental.pallas import tpu as pltpu
from jax.sharding import Mesh
from jax.sharding import PartitionSpec as P

AXES = ("section_0", "section_1", "dom_0", "dom_1", "dom_2")
SECTION = ("section_0", "section_1")
DOM = ("dom_0", "dom_1", "dom_2")
PLANE = ("dom_0", "dom_2")
TWIN = "dom_1"
LINE = ("section_0", "section_1", "dom_1")

step_scale = 0.4
epsilon = 1e-06

PEERS = 16
PERIODS_HERE = 8
LATER = tuple(range(1, 8))
CHUNK = 32
PIECE = 40

f32 = jnp.float32
VMEM = pl.BlockSpec(memory_space=pltpu.VMEM)
HBM = pl.BlockSpec(memory_space=pltpu.HBM)
SMEM = pl.BlockSpec(memory_space=pltpu.SMEM)
PARAMS = pltpu.CompilerParams(vmem_limit_bytes=32 << 20)


def shaped(*shape):
    return jax.ShapeDtypeStruct(shape, f32)


def call(kernel, outs, ins, scratch=(), places=None):
    return pl.pallas_call(
        kernel,
        out_shape=outs,
        in_specs=ins,
        out_specs=places or jax.tree.map(lambda _: VMEM, outs),
        scratch_shapes=list(scratch),
        compiler_params=PARAMS,
    )


def columns_of(ref):
    rows = jnp.concatenate([ref[:, :128], ref[:, 128:], jnp.zeros((112, 128), f32)], axis=0)
    return rows.T


def store_rows(ref, rows):
    ref[:, :128] = rows[0:8]
    ref[:, 128:] = rows[8:16]


def transposed_product(block, wide):
    return jnp.sum(block * wide, axis=0, keepdims=True)


def row_of(index_ref, t, r, k, spread):
    row = index_ref[t * 12 + r * 6 + k]
    if not spread:
        return row
    if t > 0:
        return row + (row >> 5) * (PIECE - CHUNK)
    place = row & 63
    inside = place & 3
    return (place >> 2) * PIECE + jnp.where(row < 64, inside * 8, inside + CHUNK)


def add_terms(blocks_ref, index_ref, dest_ref, t, r, wide, spread=True):
    for k in range(6):
        row = row_of(index_ref, t, r, k, spread)
        dest_ref[pl.ds(row, 1), :] += transposed_product(blocks_ref[t, r, k], wide)


def row_product(blocks_ref, index_ref, source_ref, t, r, spread=False):
    total = jnp.zeros((128, 128), f32)
    for k in range(6):
        row = row_of(index_ref, t, r, k, spread)
        total += blocks_ref[t, r, k] * source_ref[pl.ds(row, 1), :]
    return jnp.sum(total, axis=1, keepdims=True)


def adjoint_first(
    column_in, period_in, blocks_ref, dual_ref, index_ref, own_ref, carry_ref,
    column_ref, period_ref, block_rows, dual_rows, terms, arrived,
):
    get_column = pltpu.make_async_copy(column_in, column_ref, arrived.at[2])
    get_period = pltpu.make_async_copy(period_in, period_ref, arrived.at[3])
    get_column.start()
    get_period.start()
    get_blocks = pltpu.make_async_copy(blocks_ref.at[0], block_rows.at[0], arrived.at[0])
    get_dual = pltpu.make_async_copy(dual_ref, dual_rows, arrived.at[1])
    get_dual.start()
    get_blocks.start()
    terms[...] = jnp.zeros_like(terms)
    first_period = lax.axis_index(SECTION) * PERIODS_HERE
    get_column.wait()
    get_period.wait()
    for t in range(PERIODS_HERE):
        for r in range(2):
            for k in range(6):
                c = column_ref[k, r, t]
                before = first_period + t - period_ref[k, r, t]
                place = ((c >> 4) * 4 + ((c >> 1) & 3)) * 4 + ((c >> 3) & 1) * 2 + (c & 1)
                row = place + 64 * before if t == 0 else place * 8 + t - before
                index_ref[t * 12 + r * 6 + k] = row
    get_dual.wait()
    columns = columns_of(dual_rows)
    get_blocks.wait()
    for r in range(2):
        wide = jnp.broadcast_to(columns[:, r * 8 : r * 8 + 1], (128, 128))
        add_terms(block_rows, index_ref, terms, 0, r, wide, False)
    own_ref[...] = terms[0:64]
    carry_ref[...] = terms[64:128]


def adjoint_later(index_ref, blocks_ref, dual_ref, own_ref, partial_ref):
    partial_ref[...] = jnp.zeros_like(partial_ref)
    for p in range(PEERS):
        partial_ref[pl.ds(p * PIECE, 4, stride=8), :] = own_ref[p * 4 : p * 4 + 4]
    columns = columns_of(dual_ref)
    for t in LATER:
        for r in range(2):
            place = r * 8 + t
            wide = jnp.broadcast_to(columns[:, place : place + 1], (128, 128))
            add_terms(blocks_ref, index_ref, partial_ref, t, r, wide)


def add_carried(partial_in, carried_ref, partial_ref):
    partial_ref[...] = partial_in[...]
    for p in range(PEERS):
        partial_ref[pl.ds(p * PIECE + 7, 4, stride=8), :] += carried_ref[p * 4 : p * 4 + 4]


def total_of(pieces_ref):
    total = pieces_ref[0]
    for p in range(1, PEERS):
        total = total + pieces_ref[p]
    return total


def sum_and_pack(pieces_ref, primal_ref, cost_ref, pack_ref):
    pack_ref[0:CHUNK, :] = total_of(pieces_ref)[0:CHUNK]
    pack_ref[32:40, :] = primal_ref[:, :128]
    pack_ref[40:48, :] = primal_ref[:, 128:]
    pack_ref[48:56, :] = cost_ref[:, :128]
    pack_ref[56:64, :] = cost_ref[:, 128:]


def sum_and_tiles(pieces_ref, primal_one_ref, cost_ref, sum_ref, tiles_ref, tile):
    total = total_of(pieces_ref)
    sum_ref[...] = total
    last = pl.ds(7, 4, stride=8)
    tile[0:4, :] = total[32:36]
    tile[4:8, :] = sum_ref[last, :] - 0.5 * cost_ref[last, :]
    tile[8:12, :] = primal_one_ref[last, :]
    tile[12:16, :] = total[36:40]
    to_all(tiles_ref, tile[...])


def both_twins(own, other):
    first = lax.axis_index(TWIN) == 0
    return jnp.concatenate(
        [jnp.where(first, own, other), jnp.where(first, other, own)], axis=0
    )


def to_all(ref, value):
    for p in range(PEERS):
        ref[p] = value


def primal_step(weight_ref, pack_ref, other_ref, copies_ref, primal_one_ref, cost_ref, move_ref):
    tau = step_scale / jnp.full((CHUNK, 128), weight_ref[0], f32)
    product = pack_ref[0:32] + other_ref[0:32]
    start = both_twins(pack_ref[32:48], other_ref[32:48])
    cost = both_twins(pack_ref[48:64], other_ref[48:64])
    primal_one = jnp.maximum(0.0, start - tau * (cost - product))
    primal_one_ref[...] = primal_one
    cost_ref[...] = cost
    move_ref[...] = 0.5 * jnp.sum((primal_one - start) ** 2, axis=0, keepdims=True)
    to_all(copies_ref, 2.0 * primal_one - start)


def dual_later(
    index_ref, weight_ref, blocks_ref, field_ref, dual_ref, demand_ref, dual_one_ref, partial_ref, move_ref
):
    partial_ref[...] = jnp.zeros_like(partial_ref)
    sigma = step_scale * weight_ref[0]
    start = columns_of(dual_ref)
    demand = columns_of(demand_ref)
    lane = lax.broadcasted_iota(jnp.int32, (128, 128), 1)
    result = start
    for t in LATER:
        for r in range(2):
            place = r * 8 + t
            here = slice(place, place + 1)
            product = row_product(blocks_ref, index_ref, field_ref, t, r)
            dual_one = start[:, here] + sigma * (demand[:, here] - product)
            wide = jnp.broadcast_to(dual_one, (128, 128))
            result = jnp.where(lane == place, wide, result)
            add_terms(blocks_ref, index_ref, partial_ref, t, r, wide)
    move_ref[...] = jnp.sum((result - start).T ** 2, axis=0, keepdims=True)
    store_rows(dual_one_ref, result.T)


def first_rows(field_ref, carried_ref, rows):
    rows[0:64, :] = field_ref[pl.ds(0, 64, stride=8), :]
    rows[64:128, :] = carried_ref[...]


def dual_first(
    index_ref, weight_ref, blocks_ref, field_ref, carried_ref, dual_ref, demand_ref, later_ref, partial_in,
    move_x, move_a, dual_one_ref, partial_ref, rows,
):
    first_rows(field_ref, carried_ref, rows)
    partial_ref[...] = partial_in[...]
    sigma = step_scale * weight_ref[0]
    start = columns_of(dual_ref)
    demand = columns_of(demand_ref)
    later = columns_of(later_ref)
    lane = lax.broadcasted_iota(jnp.int32, (128, 128), 1)
    result = start
    for r in range(2):
        here = slice(r * 8, r * 8 + 1)
        product = row_product(blocks_ref, index_ref, rows, 0, r)
        dual_one = start[:, here] + sigma * (demand[:, here] - product)
        wide = jnp.broadcast_to(dual_one, (128, 128))
        result = jnp.where(lane == r * 8, wide, result)
        later = jnp.where(lane == r * 8, wide, later)
        add_terms(blocks_ref, index_ref, partial_ref, 0, r, wide)
    store_rows(dual_one_ref, later.T)
    move = jnp.sum((result - start).T ** 2, axis=0, keepdims=True) + move_a[...]
    moves = jnp.concatenate([move_x[...], move], 0)
    for p in range(PEERS):
        partial_ref[p * PIECE + 36 : p * PIECE + 38, :] = moves


def primal_last(
    weight_ref, tiles_ref, sum_ref, other_ref, primal_one_ref, cost_ref, copies_ref, primal_ref, steps_ref,
    gradient,
):
    section = lax.axis_index(SECTION)
    tile = tiles_ref[0, 8:16]
    for d in range(1, PEERS):
        tile = tile + tiles_ref[d, 8:16]
    move = jnp.broadcast_to(jnp.sum(tile, axis=1, keepdims=True), (8, 128))
    move_primal, move_dual = move[4:5], move[5:6]
    weight = jnp.full((1, 128), weight_ref[0], f32)
    omega = jnp.sqrt(weight * jnp.sqrt((move_dual + epsilon) / (move_primal + epsilon)))
    tau = step_scale / omega
    steps_ref[...] = jnp.broadcast_to(step_scale * omega, (8, 128))

    above = 2 * jnp.minimum(section + 1, 7)
    carried = tiles_ref[above, 0:4] + tiles_ref[above + 1, 0:4]
    gradient[...] = cost_ref[...] - (sum_ref[0:CHUNK] + other_ref[0:CHUNK])
    gradient[pl.ds(7, 4, stride=8), :] -= jnp.where(section < 7, carried, 0.0)
    primal_one = primal_one_ref[...]
    primal = jnp.maximum(0.0, primal_one - tau * gradient[...])
    primal_ref[...] = primal
    field = 2.0 * primal - primal_one

    below = 2 * jnp.maximum(section - 1, 0)
    product = tiles_ref[below, 4:8] + tiles_ref[below + 1, 4:8] + sum_ref[32:36] + other_ref[32:36]
    before_one = tiles_ref[below, 8:12]
    before = jnp.maximum(0.0, before_one + tau * product)
    before_field = 2.0 * before - before_one
    to_all(copies_ref, jnp.concatenate([field, before_field, jnp.zeros((4, 128), f32)], 0))


def last_dual(
    index_ref, blocks_ref, field_ref, steps_ref, dual_ref, demand_ref, primal_ref, primal_out, dual_out
):
    first = lax.axis_index(TWIN) == 0
    primal_out[:, :128] = jnp.where(first, primal_ref[0:8], primal_ref[16:24])
    primal_out[:, 128:] = jnp.where(first, primal_ref[8:16], primal_ref[24:32])
    lane = lax.broadcasted_iota(jnp.int32, (128, 128), 1)
    result = jnp.zeros((128, 128), f32)
    for t in range(PERIODS_HERE):
        for r in range(2):
            product = row_product(blocks_ref, index_ref, field_ref, t, r, True)
            result = jnp.where(lane == r * 8 + t, jnp.broadcast_to(product, (128, 128)), result)
    result = result.T
    sigma = steps_ref[...]
    for r in range(2):
        part = slice(r * 128, r * 128 + 128)
        dual_out[:, part] = dual_ref[:, part] + sigma * (
            demand_ref[:, part] - result[r * 8 : r * 8 + 8]
        )


def to_next(x, distance):
    route = [(i - distance, i) for i in range(8) if 0 <= i - distance < 8]
    return lax.ppermute(x, SECTION, route)


def to_twin(x):
    return lax.ppermute(x, TWIN, [(0, 1), (1, 0)])


def exchange(pieces, axis):
    return lax.all_to_all(pieces, axis, split_axis=0, concat_axis=0, tiled=True)


def in_hbm(x):
    return pltpu.with_memory_space_constraint(x, pltpu.HBM)


def on_device(
    blocks, column_index, block_period, cost_vector, demand, primal_start, dual_start, primal_weight
):
    terms = pltpu.VMEM((128, 128), f32)
    half = shaped(64, 128)
    line = shaped(1, 128)
    partials = shaped(PEERS * PIECE, 128)
    chunk = shaped(CHUNK, 128)
    copies = shaped(PEERS, CHUNK, 128)
    local = shaped(8, 256)

    index, own, carry = call(
        adjoint_first,
        [jax.ShapeDtypeStruct((96,), jnp.int32), half, half],
        [HBM] * 4,
        [
            pltpu.SMEM((6, 2, 8), jnp.int32),
            pltpu.SMEM((6, 2, 8), jnp.int32),
            pltpu.VMEM((1, 2, 6, 128, 128), f32),
            pltpu.VMEM((8, 256), f32),
            terms,
            pltpu.SemaphoreType.DMA((4,)),
        ],
        [SMEM, VMEM, VMEM],
    )(
        in_hbm(column_index.transpose(2, 1, 0)),
        in_hbm(block_period.transpose(2, 1, 0)),
        in_hbm(blocks),
        in_hbm(dual_start),
    )
    carried = to_next(carry, -1)
    partial = call(adjoint_later, partials, [SMEM, VMEM, VMEM, VMEM])(index, blocks, dual_start, own)
    partial = call(add_carried, partials, [VMEM, VMEM])(partial, carried)
    pieces = exchange(partial.reshape(PEERS, PIECE, 128), PLANE)
    pack = call(sum_and_pack, shaped(64, 128), [VMEM] * 3)(pieces, primal_start, cost_vector)
    other = to_twin(pack)
    send, primal_one, cost, move_primal = call(
        primal_step, [copies, chunk, chunk, line], [SMEM, VMEM, VMEM]
    )(primal_weight, pack, other)
    field = exchange(send, PLANE).reshape(PEERS * CHUNK, 128)
    carried = to_next(field.reshape(64, 8, 128)[:, 7], 1)
    dual_some, partial, move_a = call(
        dual_later, [local, partials, line], [SMEM, SMEM] + [VMEM] * 4
    )(index, primal_weight, blocks, field, dual_start, demand)
    dual_one, partial = call(
        dual_first, [local, partials], [SMEM, SMEM] + [VMEM] * 9, [terms]
    )(
        index, primal_weight, blocks, field, carried, dual_start, demand, dual_some, partial,
        move_primal, move_a,
    )
    pieces = exchange(partial.reshape(PEERS, PIECE, 128), PLANE)
    tile = pltpu.VMEM((16, 128), f32)
    total, tiles = call(
        sum_and_tiles, [shaped(PIECE, 128), shaped(PEERS, 16, 128)], [VMEM] * 3, [tile]
    )(pieces, primal_one, cost)
    other = to_twin(total)
    tiles = exchange(tiles, LINE)
    send, primal, steps = call(
        primal_last,
        [shaped(PEERS, PIECE, 128), chunk, shaped(8, 128)],
        [SMEM] + [VMEM] * 5,
        [pltpu.VMEM((CHUNK, 128), f32)],
    )(primal_weight, tiles, total, other, primal_one, cost)
    field = exchange(send, PLANE).reshape(PEERS * PIECE, 128)
    primal_final, dual_final = call(last_dual, [local, local], [SMEM] + [VMEM] * 6)(
        index, blocks, field, steps, dual_one, demand, primal
    )
    return primal_final, dual_final


def solution(mesh):
    finer = Mesh(mesh.devices.reshape(4, 2, 4, 2, 4), AXES)
    return jax.shard_map(
        on_device,
        mesh=finer,
        in_specs=(
            P(SECTION, DOM, None, None, None),
            P(SECTION, DOM, None),
            P(SECTION, DOM, None),
            P(SECTION, DOM),
            P(SECTION, DOM),
            P(SECTION, DOM),
            P(SECTION, DOM),
            P(),
        ),
        out_specs=(P(SECTION, DOM), P(SECTION, DOM)),
        check_vma=False,
    )
```

```python
import functools

import jax
import jax.numpy as jnp
from jax import lax
from jax.experimental import pallas as pl
from jax.experimental.pallas import tpu as pltpu
from jax.sharding import Mesh
from jax.sharding import PartitionSpec as P

AXES = ("section_0", "section_1", "dom_0", "dom_1", "dom_2")
SECTION = ("section_0", "section_1")
DOM = ("dom_0", "dom_1", "dom_2")
PLANE = ("dom_0", "dom_2")
TWIN = "dom_1"
LINE = ("section_0", "dom_1")
CORE = "section_1"

step_scale = 0.4
epsilon = 1e-06

PEERS = 16
LINE_PEERS = 8
PERIODS_HERE = 8
CHUNK = 32
PIECE = 40
HALO = slice(32, 36)

f32 = jnp.float32
VMEM = pl.BlockSpec(memory_space=pltpu.VMEM)
HBM = pl.BlockSpec(memory_space=pltpu.HBM)
SMEM = pl.BlockSpec(memory_space=pltpu.SMEM)
PARAMS = pltpu.CompilerParams(vmem_limit_bytes=32 << 20)


def shaped(*shape):
    return jax.ShapeDtypeStruct(shape, f32)


def call(kernel, outs, ins, scratch=(), places=None):
    return pl.pallas_call(
        kernel,
        out_shape=outs,
        in_specs=ins,
        out_specs=places or jax.tree.map(lambda _: VMEM, outs),
        scratch_shapes=list(scratch),
        compiler_params=PARAMS,
    )


def columns_of(ref):
    rows = jnp.concatenate([ref[:, :128], ref[:, 128:], jnp.zeros((112, 128), f32)], axis=0)
    return rows.T


def store_rows(ref, rows):
    ref[:, :128] = rows[0:8]
    ref[:, 128:] = rows[8:16]


def row_of(index_ref, t, r, k):
    return pl.ds(index_ref[t * 12 + r * 6 + k], 1)


def add_terms(blocks_ref, index_ref, dest_ref, t, r, wide):
    for k in range(6):
        term = jnp.sum(blocks_ref[t, r, k] * wide, axis=0, keepdims=True)
        dest_ref[row_of(index_ref, t, r, k), :] += term


def all_products(blocks_ref, index_ref, source_ref):
    lane = lax.broadcasted_iota(jnp.int32, (128, 128), 1)
    result = jnp.zeros((128, 128), f32)
    for t in range(PERIODS_HERE):
        for r in range(2):
            total = jnp.zeros((128, 128), f32)
            for k in range(6):
                total += blocks_ref[t, r, k] * source_ref[row_of(index_ref, t, r, k), :]
            product = jnp.sum(total, axis=1, keepdims=True)
            result = jnp.where(lane == r * 8 + t, jnp.broadcast_to(product, (128, 128)), result)
    return result


def wide_column(columns, t, r):
    place = r * 8 + t
    return jnp.broadcast_to(columns[:, place : place + 1], (128, 128))


def adjoint_start(
    column_in, period_in, blocks_in, dual_in, index_ref, partial_ref, blocks_ref,
    column_ref, period_ref, dual_ref, arrived,
):
    get_column = pltpu.make_async_copy(column_in, column_ref, arrived.at[0])
    get_period = pltpu.make_async_copy(period_in, period_ref, arrived.at[1])
    get_dual = pltpu.make_async_copy(dual_in, dual_ref, arrived.at[2])
    get_blocks = [
        pltpu.make_async_copy(blocks_in.at[t], blocks_ref.at[t], arrived.at[3 + t])
        for t in range(PERIODS_HERE)
    ]
    for copy in [get_column, get_period, get_dual] + get_blocks:
        copy.start()
    partial_ref[...] = jnp.zeros_like(partial_ref)
    first_period = lax.axis_index(SECTION) * PERIODS_HERE
    get_column.wait()
    get_period.wait()
    for t in range(PERIODS_HERE):
        for r in range(2):
            for k in range(6):
                c = column_ref[k, r, t]
                before = first_period + t - period_ref[k, r, t]
                peer = (c >> 4) * 4 + ((c >> 1) & 3)
                inside = ((c >> 3) & 1) * 2 + (c & 1)
                row = inside * 8 + t - before
                if t == 0:
                    row = jnp.where(before == 0, inside * 8, inside + CHUNK)
                index_ref[t * 12 + r * 6 + k] = peer * PIECE + row
    get_dual.wait()
    columns = columns_of(dual_ref)
    for t in range(PERIODS_HERE):
        get_blocks[t].wait()
        for r in range(2):
            add_terms(blocks_ref, index_ref, partial_ref, t, r, wide_column(columns, t, r))


def total_of(pieces_ref):
    total = pieces_ref[0]
    for p in range(1, PEERS):
        total = total + pieces_ref[p]
    return total


def to_all(ref, value, count):
    for p in range(count):
        ref[p] = value


def tile_of(tile, pieces_ref, cost_ref):
    tile[0:PIECE, :] = total_of(pieces_ref)
    own = pl.multiple_of(lax.axis_index(TWIN) * 16, 16)
    tile[pl.ds(own, 8), :] -= cost_ref[:, :128]
    tile[pl.ds(own + 8, 8), :] -= cost_ref[:, 128:]


def sum_first(pieces_ref, cost_ref, primal_ref, tiles_ref, tile):
    tile_of(tile, pieces_ref, cost_ref)
    tile[40:48, :] = primal_ref[:, :128]
    tile[48:56, :] = primal_ref[:, 128:]
    to_all(tiles_ref, tile[...], LINE_PEERS)


def sum_second(pieces_ref, cost_ref, tiles_ref, tile):
    tile_of(tile, pieces_ref, cost_ref)
    to_all(tiles_ref, tile[...], LINE_PEERS)


def for_other_core(tiles_ref, pack_ref):
    chip = lax.axis_index("section_0")
    core = lax.axis_index(CORE)
    above = 2 * jnp.minimum(chip + 1 - core, 3)
    below = 2 * jnp.maximum(chip - core, 0)
    last = pl.ds(7, 4, stride=8)
    pack_ref[...] = jnp.zeros_like(pack_ref)
    pack_ref[0:4, :] = tiles_ref[above, HALO] + tiles_ref[above + 1, HALO]
    pack_ref[4:8, :] = tiles_ref[below, last] + tiles_ref[below + 1, last]
    if tiles_ref.shape[1] > PIECE:
        late = pl.ds(47, 2, stride=8)
        pack_ref[8:10, :] = tiles_ref[below, late]
        pack_ref[10:12, :] = tiles_ref[below + 1, late]
    moves = tiles_ref[0, 36:40]
    for d in range(1, LINE_PEERS):
        moves = moves + tiles_ref[d, 36:40]
    pack_ref[12:16, :] = moves


def descents(tiles_ref, other_ref, descent):
    section = lax.axis_index(SECTION)
    here = 2 * lax.axis_index("section_0")
    descent[...] = tiles_ref[here, 0:CHUNK] + tiles_ref[here + 1, 0:CHUNK]
    descent[pl.ds(7, 4, stride=8), :] += jnp.where(section < 7, other_ref[0:4], 0.0)
    before = other_ref[4:8] + tiles_ref[here, HALO] + tiles_ref[here + 1, HALO]
    return descent[...], before


def send_field(copies_ref, field, before):
    to_all(copies_ref, jnp.concatenate([field, before, jnp.zeros((4, 128), f32)], 0), PEERS)


def primal_step(
    weight_ref, tiles_ref, other_ref, copies_ref, primal_one_ref, before_one_ref, move_ref, descent
):
    tau = step_scale / jnp.full((1, 128), weight_ref[0], f32)
    along, along_before = descents(tiles_ref, other_ref, descent)
    here = 2 * lax.axis_index("section_0")
    start = jnp.concatenate([tiles_ref[here, 40:56], tiles_ref[here + 1, 40:56]], 0)
    start_before = other_ref[8:12]
    primal_one = jnp.maximum(0.0, start + tau * along)
    before_one = jnp.maximum(0.0, start_before + tau * along_before)
    primal_one_ref[...] = primal_one
    before_one_ref[...] = before_one
    move_ref[...] = 0.5 * jnp.sum((primal_one - start) ** 2, axis=0, keepdims=True)
    send_field(copies_ref, 2.0 * primal_one - start, 2.0 * before_one - start_before)


def dual_step(
    index_ref, weight_ref, blocks_ref, field_ref, dual_ref, demand_ref, move_x, dual_one_ref, partial_ref
):
    partial_ref[...] = jnp.zeros_like(partial_ref)
    sigma = step_scale * weight_ref[0]
    start = columns_of(dual_ref)
    demand = columns_of(demand_ref)
    product = all_products(blocks_ref, index_ref, field_ref)
    dual_one = start + sigma * (demand - product)
    for t in range(PERIODS_HERE):
        for r in range(2):
            add_terms(blocks_ref, index_ref, partial_ref, t, r, wide_column(dual_one, t, r))
    move = jnp.sum((dual_one - start).T ** 2, axis=0, keepdims=True)
    moves = jnp.concatenate([move_x[...], move], 0)
    for p in range(PEERS):
        partial_ref[p * PIECE + 36 : p * PIECE + 38, :] = moves
    store_rows(dual_one_ref, dual_one.T)


def primal_last(
    weight_ref, tiles_ref, other_ref, primal_one_ref, before_one_ref, copies_ref, primal_ref, steps_ref, descent
):
    moves = other_ref[8:16]
    for d in range(LINE_PEERS):
        moves = moves + tiles_ref[d, 32:40]
    move = jnp.broadcast_to(jnp.sum(moves, axis=1, keepdims=True), (8, 128))
    move_primal, move_dual = move[4:5], move[5:6]
    weight = jnp.full((1, 128), weight_ref[0], f32)
    omega = jnp.sqrt(weight * jnp.sqrt((move_dual + epsilon) / (move_primal + epsilon)))
    tau = step_scale / omega
    steps_ref[...] = jnp.broadcast_to(step_scale * omega, (8, 128))
    along, along_before = descents(tiles_ref, other_ref, descent)
    primal_one = primal_one_ref[...]
    before_one = before_one_ref[...]
    primal = jnp.maximum(0.0, primal_one + tau * along)
    before = jnp.maximum(0.0, before_one + tau * along_before)
    primal_ref[...] = primal
    send_field(copies_ref, 2.0 * primal - primal_one, 2.0 * before - before_one)


def dual_last(
    index_ref, blocks_ref, field_ref, steps_ref, dual_ref, demand_ref, primal_ref, primal_out, dual_out
):
    own = pl.multiple_of(lax.axis_index(TWIN) * 16, 16)
    primal_out[:, :128] = primal_ref[pl.ds(own, 8), :]
    primal_out[:, 128:] = primal_ref[pl.ds(own + 8, 8), :]
    result = all_products(blocks_ref, index_ref, field_ref).T
    sigma = steps_ref[...]
    for r in range(2):
        part = slice(r * 128, r * 128 + 128)
        dual_out[:, part] = dual_ref[:, part] + sigma * (
            demand_ref[:, part] - result[r * 8 : r * 8 + 8]
        )


def to_other_core(x):
    return lax.ppermute(x, CORE, [(0, 1), (1, 0)])


def exchange(pieces, axis):
    return lax.all_to_all(pieces, axis, split_axis=0, concat_axis=0, tiled=True)


def in_hbm(x):
    return pltpu.with_memory_space_constraint(x, pltpu.HBM)


def on_device(
    blocks, column_index, block_period, cost_vector, demand, primal_start, dual_start, primal_weight
):
    partials = shaped(PEERS * PIECE, 128)
    pieces = (PEERS, PIECE, 128)
    chunk = shaped(CHUNK, 128)
    local = shaped(8, 256)
    pack = shaped(16, 128)
    rows = pltpu.VMEM((CHUNK, 128), f32)

    index, partial, kept = call(
        adjoint_start,
        [jax.ShapeDtypeStruct((96,), jnp.int32), partials, shaped(*blocks.shape)],
        [HBM] * 4,
        [
            pltpu.SMEM((6, 2, 8), jnp.int32),
            pltpu.SMEM((6, 2, 8), jnp.int32),
            pltpu.VMEM((8, 256), f32),
            pltpu.SemaphoreType.DMA((11,)),
        ],
        [SMEM, VMEM, VMEM],
    )(
        in_hbm(column_index.transpose(2, 1, 0)),
        in_hbm(block_period.transpose(2, 1, 0)),
        in_hbm(blocks),
        in_hbm(dual_start),
    )
    kept = pltpu.with_memory_space_constraint(kept, pltpu.VMEM)
    arrived = exchange(partial.reshape(pieces), PLANE)
    tiles = call(
        sum_first, shaped(LINE_PEERS, 56, 128), [VMEM] * 3, [pltpu.VMEM((56, 128), f32)]
    )(arrived, cost_vector, primal_start)
    tiles = exchange(tiles, LINE)
    other = to_other_core(call(for_other_core, pack, [VMEM])(tiles))
    send, primal_one, before_one, move_primal = call(
        primal_step,
        [shaped(*pieces), chunk, shaped(4, 128), shaped(1, 128)],
        [SMEM, VMEM, VMEM],
        [rows],
    )(primal_weight, tiles, other)
    field = exchange(send, PLANE).reshape(PEERS * PIECE, 128)
    dual_one, partial = call(dual_step, [local, partials], [SMEM, SMEM] + [VMEM] * 5)(
        index, primal_weight, kept, field, dual_start, demand, move_primal
    )
    arrived = exchange(partial.reshape(pieces), PLANE)
    tiles = call(sum_second, shaped(LINE_PEERS, PIECE, 128), [VMEM] * 2, [pltpu.VMEM((PIECE, 128), f32)])(
        arrived, cost_vector
    )
    tiles = exchange(tiles, LINE)
    other = to_other_core(call(for_other_core, pack, [VMEM])(tiles))
    send, primal, steps = call(
        primal_last, [shaped(*pieces), chunk, shaped(8, 128)], [SMEM] + [VMEM] * 4, [rows]
    )(primal_weight, tiles, other, primal_one, before_one)
    field = exchange(send, PLANE).reshape(PEERS * PIECE, 128)
    primal_final, dual_final = call(dual_last, [local, local], [SMEM] + [VMEM] * 6)(
        index, kept, field, steps, dual_one, demand, primal
    )
    return primal_final, dual_final


def solution(mesh):
    finer = Mesh(mesh.devices.reshape(4, 2, 4, 2, 4), AXES)
    return jax.shard_map(
        on_device,
        mesh=finer,
        in_specs=(
            P(SECTION, DOM, None, None, None),
            P(SECTION, DOM, None),
            P(SECTION, DOM, None),
            P(SECTION, DOM),
            P(SECTION, DOM),
            P(SECTION, DOM),
            P(SECTION, DOM),
            P(),
        ),
        out_specs=(P(SECTION, DOM), P(SECTION, DOM)),
        check_vma=False,
    )
```

```python
import functools

import jax
import jax.numpy as jnp
from jax import lax
from jax.experimental import pallas as pl
from jax.experimental.pallas import tpu as pltpu
from jax.sharding import Mesh
from jax.sharding import PartitionSpec as P

AXES = ("section_0", "section_1", "dom_0", "dom_1", "dom_2")
SECTION = ("section_0", "section_1")
DOM = ("dom_0", "dom_1", "dom_2")
PLANE = ("dom_0", "dom_2")
TWIN = "dom_1"
LINE = ("section_0", "dom_1")
CORE = "section_1"

step_scale = 0.4
epsilon = 1e-06

PEERS = 16
LINE_PEERS = 8
PERIODS_HERE = 8
CHUNK = 32
PIECE = 40
HALO = slice(32, 36)

f32 = jnp.float32
VMEM = pl.BlockSpec(memory_space=pltpu.VMEM)
HBM = pl.BlockSpec(memory_space=pltpu.HBM)
SMEM = pl.BlockSpec(memory_space=pltpu.SMEM)
PARAMS = pltpu.CompilerParams(vmem_limit_bytes=32 << 20)


def shaped(*shape):
    return jax.ShapeDtypeStruct(shape, f32)


def call(kernel, outs, ins, scratch=()):
    return pl.pallas_call(
        kernel,
        out_shape=outs,
        in_specs=ins,
        out_specs=jax.tree.map(lambda _: VMEM, outs),
        scratch_shapes=list(scratch),
        compiler_params=PARAMS,
    )


def columns_of(ref):
    rows = jnp.concatenate([ref[:, :128], ref[:, 128:], jnp.zeros((112, 128), f32)], axis=0)
    return rows.T


def store_rows(ref, rows):
    ref[:, :128] = rows[0:8]
    ref[:, 128:] = rows[8:16]


def row_of(index_ref, t, r, k):
    return pl.ds(index_ref[t * 12 + r * 6 + k], 1)


def add_terms(blocks_ref, index_ref, dest_ref, t, r, wide):
    for k in range(6):
        term = jnp.sum(blocks_ref[t, r, k] * wide, axis=0, keepdims=True)
        dest_ref[row_of(index_ref, t, r, k), :] += term


def all_products(blocks_ref, index_ref, source_ref):
    lane = lax.broadcasted_iota(jnp.int32, (128, 128), 1)
    result = jnp.zeros((128, 128), f32)
    for t in range(PERIODS_HERE):
        for r in range(2):
            total = jnp.zeros((128, 128), f32)
            for k in range(6):
                total += blocks_ref[t, r, k] * source_ref[row_of(index_ref, t, r, k), :]
            product = jnp.sum(total, axis=1, keepdims=True)
            result = jnp.where(lane == r * 8 + t, jnp.broadcast_to(product, (128, 128)), result)
    return result


def wide_column(columns, t, r):
    place = r * 8 + t
    return jnp.broadcast_to(columns[:, place : place + 1], (128, 128))


def fill_index(column_ref, period_ref, index_ref, t):
    for r in range(2):
        for k in range(6):
            c = column_ref[k, r, t]
            before = lax.axis_index(SECTION) * PERIODS_HERE + t - period_ref[k, r, t]
            peer = (c >> 4) * 4 + ((c >> 1) & 3)
            inside = ((c >> 3) & 1) * 2 + (c & 1)
            row = inside * 8 + t - before
            if t == 0:
                row = jnp.where(before == 0, inside * 8, inside + CHUNK)
            index_ref[t * 12 + r * 6 + k] = peer * PIECE + row


def adjoint_start(
    column_in, period_in, blocks_in, dual_in, index_out, partial_ref, blocks_ref,
    column_ref, period_ref, index_ref, dual_ref, arrived,
):
    get_column = pltpu.make_async_copy(column_in, column_ref, arrived.at[0])
    get_period = pltpu.make_async_copy(period_in, period_ref, arrived.at[1])
    get_dual = pltpu.make_async_copy(dual_in, dual_ref, arrived.at[2])
    get_blocks = [
        pltpu.make_async_copy(blocks_in.at[t], blocks_ref.at[t], arrived.at[3 + t])
        for t in range(PERIODS_HERE)
    ]
    for copy in [get_column, get_period, get_dual] + get_blocks:
        copy.start()
    partial_ref[...] = jnp.zeros_like(partial_ref)
    get_dual.wait()
    columns = columns_of(dual_ref)
    get_column.wait()
    get_period.wait()
    for t in range(PERIODS_HERE):
        fill_index(column_ref, period_ref, index_ref, t)
    put_index = pltpu.make_async_copy(index_ref, index_out, arrived.at[11])
    put_index.start()
    for t in range(PERIODS_HERE):
        get_blocks[t].wait()
        for r in range(2):
            add_terms(blocks_ref, index_ref, partial_ref, t, r, wide_column(columns, t, r))
    put_index.wait()


def total_of(pieces_ref):
    total = pieces_ref[0]
    for p in range(1, PEERS):
        total = total + pieces_ref[p]
    return total


def to_all(ref, value, count):
    for p in range(count):
        ref[p] = value


def tile_of(tile, pieces_ref, cost_ref):
    tile[0:PIECE, :] = total_of(pieces_ref)
    own = pl.multiple_of(lax.axis_index(TWIN) * 16, 16)
    tile[pl.ds(own, 8), :] -= cost_ref[:, :128]
    tile[pl.ds(own + 8, 8), :] -= cost_ref[:, 128:]


def sum_first(pieces_ref, cost_ref, primal_ref, tiles_ref, tile):
    tile_of(tile, pieces_ref, cost_ref)
    tile[36:37, :] = primal_ref[7:8, :128]
    tile[37:38, :] = primal_ref[7:8, 128:]
    to_all(tiles_ref, tile[...], LINE_PEERS)


def sum_second(pieces_ref, cost_ref, tiles_ref, tile):
    tile_of(tile, pieces_ref, cost_ref)
    to_all(tiles_ref, tile[...], LINE_PEERS)


def for_other_core(tiles_ref, pack_ref):
    chip = lax.axis_index("section_0")
    core = lax.axis_index(CORE)
    above = 2 * jnp.minimum(chip + 1 - core, 3)
    below = 2 * jnp.maximum(chip - core, 0)
    last = pl.ds(7, 4, stride=8)
    pack_ref[...] = jnp.zeros_like(pack_ref)
    pack_ref[0:4, :] = tiles_ref[above, HALO] + tiles_ref[above + 1, HALO]
    pack_ref[4:8, :] = tiles_ref[below, last] + tiles_ref[below + 1, last]
    pack_ref[8:10, :] = tiles_ref[below, 36:38]
    pack_ref[10:12, :] = tiles_ref[below + 1, 36:38]
    moves = tiles_ref[0, 36:40]
    for d in range(1, LINE_PEERS):
        moves = moves + tiles_ref[d, 36:40]
    pack_ref[12:16, :] = moves


def descents(tiles_ref, other_ref, descent):
    section = lax.axis_index(SECTION)
    here = 2 * lax.axis_index("section_0")
    descent[...] = tiles_ref[here, 0:CHUNK] + tiles_ref[here + 1, 0:CHUNK]
    descent[pl.ds(7, 4, stride=8), :] += jnp.where(section < 7, other_ref[0:4], 0.0)
    before = other_ref[4:8] + tiles_ref[here, HALO] + tiles_ref[here + 1, HALO]
    return descent[...], before


def send_field(copies_ref, field, before):
    to_all(copies_ref, jnp.concatenate([field, before, jnp.zeros((4, 128), f32)], 0), PEERS)


def primal_step(
    weight_ref, tiles_ref, other_ref, primal_ref, twin_ref, copies_ref, primal_one_ref, before_one_ref, move_ref,
    descent,
):
    tau = step_scale / jnp.full((1, 128), weight_ref[0], f32)
    along, along_before = descents(tiles_ref, other_ref, descent)
    first = lax.axis_index(TWIN) == 0
    own, twin = (
        jnp.concatenate([ref[:, :128], ref[:, 128:]], 0) for ref in (primal_ref, twin_ref)
    )
    start = jnp.concatenate([jnp.where(first, own, twin), jnp.where(first, twin, own)], 0)
    start_before = other_ref[8:12]
    primal_one = jnp.maximum(0.0, start + tau * along)
    before_one = jnp.maximum(0.0, start_before + tau * along_before)
    primal_one_ref[...] = primal_one
    before_one_ref[...] = before_one
    move_ref[...] = 0.5 * jnp.sum((primal_one - start) ** 2, axis=0, keepdims=True)
    send_field(copies_ref, 2.0 * primal_one - start, 2.0 * before_one - start_before)


def dual_step(
    index_in, weight_ref, blocks_ref, field_ref, dual_ref, demand_ref, move_x, dual_one_ref, partial_ref,
    index_ref, arrived,
):
    get_index = pltpu.make_async_copy(index_in, index_ref, arrived)
    get_index.start()
    partial_ref[...] = jnp.zeros_like(partial_ref)
    sigma = step_scale * weight_ref[0]
    start = columns_of(dual_ref)
    demand = columns_of(demand_ref)
    get_index.wait()
    product = all_products(blocks_ref, index_ref, field_ref)
    dual_one = start + sigma * (demand - product)
    for t in range(PERIODS_HERE):
        for r in range(2):
            add_terms(blocks_ref, index_ref, partial_ref, t, r, wide_column(dual_one, t, r))
    move = jnp.sum((dual_one - start).T ** 2, axis=0, keepdims=True)
    moves = jnp.concatenate([move_x[...], move], 0)
    for p in range(PEERS):
        partial_ref[p * PIECE + 36 : p * PIECE + 38, :] = moves
    store_rows(dual_one_ref, dual_one.T)


def primal_last(
    weight_ref, tiles_ref, other_ref, primal_one_ref, before_one_ref, copies_ref, primal_ref, steps_ref, descent
):
    moves = other_ref[8:16]
    for d in range(LINE_PEERS):
        moves = moves + tiles_ref[d, 32:40]
    move = jnp.broadcast_to(jnp.sum(moves, axis=1, keepdims=True), (8, 128))
    move_primal, move_dual = move[4:5], move[5:6]
    weight = jnp.full((1, 128), weight_ref[0], f32)
    omega = jnp.sqrt(weight * jnp.sqrt((move_dual + epsilon) / (move_primal + epsilon)))
    tau = step_scale / omega
    steps_ref[...] = jnp.broadcast_to(step_scale * omega, (8, 128))
    along, along_before = descents(tiles_ref, other_ref, descent)
    primal_one = primal_one_ref[...]
    before_one = before_one_ref[...]
    primal = jnp.maximum(0.0, primal_one + tau * along)
    before = jnp.maximum(0.0, before_one + tau * along_before)
    primal_ref[...] = primal
    send_field(copies_ref, 2.0 * primal - primal_one, 2.0 * before - before_one)


def dual_last(
    index_in, blocks_ref, field_ref, steps_ref, dual_ref, demand_ref, primal_ref, primal_out, dual_out,
    index_ref, arrived,
):
    get_index = pltpu.make_async_copy(index_in, index_ref, arrived)
    get_index.start()
    own = pl.multiple_of(lax.axis_index(TWIN) * 16, 16)
    primal_out[:, :128] = primal_ref[pl.ds(own, 8), :]
    primal_out[:, 128:] = primal_ref[pl.ds(own + 8, 8), :]
    get_index.wait()
    result = all_products(blocks_ref, index_ref, field_ref).T
    sigma = steps_ref[...]
    for r in range(2):
        part = slice(r * 128, r * 128 + 128)
        dual_out[:, part] = dual_ref[:, part] + sigma * (
            demand_ref[:, part] - result[r * 8 : r * 8 + 8]
        )


def to_other_core(x):
    return lax.ppermute(x, CORE, [(0, 1), (1, 0)])


def exchange(pieces, axis):
    return lax.all_to_all(pieces, axis, split_axis=0, concat_axis=0, tiled=True)


def in_hbm(x):
    return pltpu.with_memory_space_constraint(x, pltpu.HBM)


def on_device(
    blocks, column_index, block_period, cost_vector, demand, primal_start, dual_start, primal_weight
):
    partials = shaped(PEERS * PIECE, 128)
    pieces = (PEERS, PIECE, 128)
    chunk = shaped(CHUNK, 128)
    local = shaped(8, 256)
    pack = shaped(16, 128)
    rows = pltpu.VMEM((CHUNK, 128), f32)
    tile = shaped(LINE_PEERS, PIECE, 128)
    rows_of_tile = [pltpu.VMEM((PIECE, 128), f32)]
    primal_twin = lax.ppermute(primal_start, TWIN, [(0, 1), (1, 0)])

    places = [pltpu.SMEM((96,), jnp.int32), pltpu.SemaphoreType.DMA(())]
    index, partial, kept = call(
        adjoint_start,
        [jax.ShapeDtypeStruct((96,), jnp.int32), partials, shaped(*blocks.shape)],
        [HBM] * 4,
        [
            pltpu.SMEM((6, 2, 8), jnp.int32),
            pltpu.SMEM((6, 2, 8), jnp.int32),
            places[0],
            pltpu.VMEM((8, 256), f32),
            pltpu.SemaphoreType.DMA((12,)),
        ],
    )(
        in_hbm(column_index.transpose(2, 1, 0)),
        in_hbm(block_period.transpose(2, 1, 0)),
        in_hbm(blocks),
        in_hbm(dual_start),
    )
    kept = pltpu.with_memory_space_constraint(kept, pltpu.VMEM)
    arrived = exchange(partial.reshape(pieces), PLANE)
    tiles = call(sum_first, tile, [VMEM] * 3, rows_of_tile)(arrived, cost_vector, primal_start)
    tiles = exchange(tiles, LINE)
    other = to_other_core(call(for_other_core, pack, [VMEM])(tiles))
    send, primal_one, before_one, move_primal = call(
        primal_step,
        [shaped(*pieces), chunk, shaped(4, 128), shaped(1, 128)],
        [SMEM] + [VMEM] * 4,
        [rows],
    )(primal_weight, tiles, other, primal_start, primal_twin)
    field = exchange(send, PLANE).reshape(PEERS * PIECE, 128)
    dual_one, partial = call(
        dual_step, [local, partials], [VMEM, SMEM] + [VMEM] * 5, places
    )(
        index, primal_weight, kept, field, dual_start, demand, move_primal
    )
    arrived = exchange(partial.reshape(pieces), PLANE)
    tiles = call(sum_second, tile, [VMEM] * 2, rows_of_tile)(arrived, cost_vector)
    tiles = exchange(tiles, LINE)
    other = to_other_core(call(for_other_core, pack, [VMEM])(tiles))
    send, primal, steps = call(
        primal_last, [shaped(*pieces), chunk, shaped(8, 128)], [SMEM] + [VMEM] * 4, [rows]
    )(primal_weight, tiles, other, primal_one, before_one)
    field = exchange(send, PLANE).reshape(PEERS * PIECE, 128)
    primal_final, dual_final = call(dual_last, [local, local], [VMEM] * 7, places)(
        index, kept, field, steps, dual_one, demand, primal
    )
    return primal_final, dual_final


def solution(mesh):
    finer = Mesh(mesh.devices.reshape(4, 2, 4, 2, 4), AXES)
    return jax.shard_map(
        on_device,
        mesh=finer,
        in_specs=(
            P(SECTION, DOM, None, None, None),
            P(SECTION, DOM, None),
            P(SECTION, DOM, None),
            P(SECTION, DOM),
            P(SECTION, DOM),
            P(SECTION, DOM),
            P(SECTION, DOM),
            P(),
        ),
        out_specs=(P(SECTION, DOM), P(SECTION, DOM)),
        check_vma=False,
    )
```

```python
import functools

import jax
import jax.numpy as jnp
from jax import lax
from jax.experimental import pallas as pl
from jax.experimental.pallas import tpu as pltpu
from jax.sharding import Mesh
from jax.sharding import PartitionSpec as P

AXES = ("section_0", "section_1", "dom_00", "dom_01", "dom_1", "dom_20", "dom_21")
SECTION = ("section_0", "section_1")
DOM = ("dom_00", "dom_01", "dom_1", "dom_20", "dom_21")
PLANE = ("dom_21", "dom_20", "dom_00", "dom_01")
TWIN = "dom_1"
LINE = ("section_0", "dom_1")
CORE = "section_1"

step_scale = 0.4
epsilon = 1e-06

PEERS = 16
LINE_PEERS = 8
PERIODS_HERE = 8
CHUNK = 32
PIECE = 40
HALO = slice(32, 36)

f32 = jnp.float32
VMEM = pl.BlockSpec(memory_space=pltpu.VMEM)
HBM = pl.BlockSpec(memory_space=pltpu.HBM)
SMEM = pl.BlockSpec(memory_space=pltpu.SMEM)
PARAMS = pltpu.CompilerParams(vmem_limit_bytes=32 << 20)


def shaped(*shape):
    return jax.ShapeDtypeStruct(shape, f32)


def call(kernel, outs, ins, scratch=()):
    return pl.pallas_call(
        kernel,
        out_shape=outs,
        in_specs=ins,
        out_specs=jax.tree.map(lambda _: VMEM, outs),
        scratch_shapes=list(scratch),
        compiler_params=PARAMS,
    )


def columns_of(ref):
    rows = jnp.concatenate([ref[:, :128], ref[:, 128:], jnp.zeros((112, 128), f32)], axis=0)
    return rows.T


def store_rows(ref, rows):
    ref[:, :128] = rows[0:8]
    ref[:, 128:] = rows[8:16]


def row_of(index_ref, t, r, k):
    return pl.ds(index_ref[t * 12 + r * 6 + k], 1)


def add_terms(blocks_ref, index_ref, dest_ref, t, r, wide):
    for k in range(6):
        term = jnp.sum(blocks_ref[t, r, k] * wide, axis=0, keepdims=True)
        dest_ref[row_of(index_ref, t, r, k), :] += term


def all_products(blocks_ref, index_ref, source_ref):
    lane = lax.broadcasted_iota(jnp.int32, (128, 128), 1)
    result = jnp.zeros((128, 128), f32)
    for t in range(PERIODS_HERE):
        for r in range(2):
            total = jnp.zeros((128, 128), f32)
            for k in range(6):
                total += blocks_ref[t, r, k] * source_ref[row_of(index_ref, t, r, k), :]
            product = jnp.sum(total, axis=1, keepdims=True)
            result = jnp.where(lane == r * 8 + t, jnp.broadcast_to(product, (128, 128)), result)
    return result


def wide_column(columns, t, r):
    place = r * 8 + t
    return jnp.broadcast_to(columns[:, place : place + 1], (128, 128))


def fill_index(column_ref, period_ref, index_ref, t):
    for r in range(2):
        for k in range(6):
            c = column_ref[k, r, t]
            before = lax.axis_index(SECTION) * PERIODS_HERE + t - period_ref[k, r, t]
            peer = ((c >> 1) & 1) * 8 + ((c >> 2) & 1) * 4 + ((c >> 5) & 1) * 2 + ((c >> 4) & 1) * 1
            inside = ((c >> 3) & 1) * 2 + (c & 1)
            row = inside * 8 + t - before
            if t == 0:
                row = jnp.where(before == 0, inside * 8, inside + CHUNK)
            index_ref[t * 12 + r * 6 + k] = peer * PIECE + row


def adjoint_start(
    column_in, period_in, blocks_in, dual_in, index_out, partial_ref, blocks_ref,
    column_ref, period_ref, index_ref, dual_ref, arrived,
):
    get_column = pltpu.make_async_copy(column_in, column_ref, arrived.at[0])
    get_period = pltpu.make_async_copy(period_in, period_ref, arrived.at[1])
    get_dual = pltpu.make_async_copy(dual_in, dual_ref, arrived.at[2])
    get_blocks = [
        pltpu.make_async_copy(blocks_in.at[t], blocks_ref.at[t], arrived.at[3 + t])
        for t in range(PERIODS_HERE)
    ]
    for copy in [get_column, get_period, get_dual] + get_blocks:
        copy.start()
    partial_ref[...] = jnp.zeros_like(partial_ref)
    get_dual.wait()
    columns = columns_of(dual_ref)
    get_column.wait()
    get_period.wait()
    for t in range(PERIODS_HERE):
        fill_index(column_ref, period_ref, index_ref, t)
    put_index = pltpu.make_async_copy(index_ref, index_out, arrived.at[11])
    put_index.start()
    for t in range(PERIODS_HERE):
        get_blocks[t].wait()
        for r in range(2):
            add_terms(blocks_ref, index_ref, partial_ref, t, r, wide_column(columns, t, r))
    put_index.wait()


def total_of(pieces_ref):
    total = pieces_ref[0]
    for p in range(1, PEERS):
        total = total + pieces_ref[p]
    return total


def to_all(ref, value, count):
    for p in range(count):
        ref[p] = value


def tile_of(tile, pieces_ref, cost_ref):
    tile[0:PIECE, :] = total_of(pieces_ref)
    own = pl.multiple_of(lax.axis_index(TWIN) * 16, 16)
    tile[pl.ds(own, 8), :] -= cost_ref[:, :128]
    tile[pl.ds(own + 8, 8), :] -= cost_ref[:, 128:]


def sum_first(pieces_ref, cost_ref, primal_ref, tiles_ref, tile):
    tile_of(tile, pieces_ref, cost_ref)
    tile[40:48, :] = primal_ref[:, :128]
    tile[48:56, :] = primal_ref[:, 128:]
    to_all(tiles_ref, tile[...], LINE_PEERS)


def sum_second(pieces_ref, cost_ref, tiles_ref, tile):
    tile_of(tile, pieces_ref, cost_ref)
    to_all(tiles_ref, tile[...], LINE_PEERS)


def for_other_core(tiles_ref, pack_ref):
    chip = lax.axis_index("section_0")
    core = lax.axis_index(CORE)
    above = 2 * jnp.minimum(chip + 1 - core, 3)
    below = 2 * jnp.maximum(chip - core, 0)
    last = pl.ds(7, 4, stride=8)
    pack_ref[...] = jnp.zeros_like(pack_ref)
    pack_ref[0:4, :] = tiles_ref[above, HALO] + tiles_ref[above + 1, HALO]
    pack_ref[4:8, :] = tiles_ref[below, last] + tiles_ref[below + 1, last]
    if tiles_ref.shape[1] > PIECE:
        late = pl.ds(47, 2, stride=8)
        pack_ref[8:10, :] = tiles_ref[below, late]
        pack_ref[10:12, :] = tiles_ref[below + 1, late]
    moves = tiles_ref[0, 36:40]
    for d in range(1, LINE_PEERS):
        moves = moves + tiles_ref[d, 36:40]
    pack_ref[12:16, :] = moves


def descents(tiles_ref, other_ref, descent):
    section = lax.axis_index(SECTION)
    here = 2 * lax.axis_index("section_0")
    descent[...] = tiles_ref[here, 0:CHUNK] + tiles_ref[here + 1, 0:CHUNK]
    descent[pl.ds(7, 4, stride=8), :] += jnp.where(section < 7, other_ref[0:4], 0.0)
    before = other_ref[4:8] + tiles_ref[here, HALO] + tiles_ref[here + 1, HALO]
    return descent[...], before


def send_field(copies_ref, field, before):
    to_all(copies_ref, jnp.concatenate([field, before, jnp.zeros((4, 128), f32)], 0), PEERS)


def primal_step(
    weight_ref, tiles_ref, other_ref, copies_ref, primal_one_ref, before_one_ref, move_ref, descent
):
    tau = step_scale / jnp.full((1, 128), weight_ref[0], f32)
    along, along_before = descents(tiles_ref, other_ref, descent)
    here = 2 * lax.axis_index("section_0")
    start = jnp.concatenate([tiles_ref[here, 40:56], tiles_ref[here + 1, 40:56]], 0)
    start_before = other_ref[8:12]
    primal_one = jnp.maximum(0.0, start + tau * along)
    before_one = jnp.maximum(0.0, start_before + tau * along_before)
    primal_one_ref[...] = primal_one
    before_one_ref[...] = before_one
    move_ref[...] = 0.5 * jnp.sum((primal_one - start) ** 2, axis=0, keepdims=True)
    send_field(copies_ref, 2.0 * primal_one - start, 2.0 * before_one - start_before)


def dual_step(
    index_in, weight_ref, blocks_ref, field_ref, dual_ref, demand_ref, move_x, dual_one_ref, partial_ref,
    index_ref, arrived,
):
    get_index = pltpu.make_async_copy(index_in, index_ref, arrived)
    get_index.start()
    partial_ref[...] = jnp.zeros_like(partial_ref)
    sigma = step_scale * weight_ref[0]
    start = columns_of(dual_ref)
    demand = columns_of(demand_ref)
    get_index.wait()
    product = all_products(blocks_ref, index_ref, field_ref)
    dual_one = start + sigma * (demand - product)
    for t in range(PERIODS_HERE):
        for r in range(2):
            add_terms(blocks_ref, index_ref, partial_ref, t, r, wide_column(dual_one, t, r))
    move = jnp.sum((dual_one - start).T ** 2, axis=0, keepdims=True)
    moves = jnp.concatenate([move_x[...], move], 0)
    for p in range(PEERS):
        partial_ref[p * PIECE + 36 : p * PIECE + 38, :] = moves
    store_rows(dual_one_ref, dual_one.T)


def primal_last(
    weight_ref, tiles_ref, other_ref, primal_one_ref, before_one_ref, copies_ref, primal_ref, steps_ref, descent
):
    moves = other_ref[8:16]
    for d in range(LINE_PEERS):
        moves = moves + tiles_ref[d, 32:40]
    move = jnp.broadcast_to(jnp.sum(moves, axis=1, keepdims=True), (8, 128))
    move_primal, move_dual = move[4:5], move[5:6]
    weight = jnp.full((1, 128), weight_ref[0], f32)
    omega = jnp.sqrt(weight * jnp.sqrt((move_dual + epsilon) / (move_primal + epsilon)))
    tau = step_scale / omega
    steps_ref[...] = jnp.broadcast_to(step_scale * omega, (8, 128))
    along, along_before = descents(tiles_ref, other_ref, descent)
    primal_one = primal_one_ref[...]
    before_one = before_one_ref[...]
    primal = jnp.maximum(0.0, primal_one + tau * along)
    before = jnp.maximum(0.0, before_one + tau * along_before)
    primal_ref[...] = primal
    send_field(copies_ref, 2.0 * primal - primal_one, 2.0 * before - before_one)


def dual_last(
    index_in, blocks_ref, field_ref, steps_ref, dual_ref, demand_ref, primal_ref, primal_out, dual_out,
    index_ref, arrived,
):
    get_index = pltpu.make_async_copy(index_in, index_ref, arrived)
    get_index.start()
    own = pl.multiple_of(lax.axis_index(TWIN) * 16, 16)
    primal_out[:, :128] = primal_ref[pl.ds(own, 8), :]
    primal_out[:, 128:] = primal_ref[pl.ds(own + 8, 8), :]
    get_index.wait()
    result = all_products(blocks_ref, index_ref, field_ref).T
    sigma = steps_ref[...]
    for r in range(2):
        part = slice(r * 128, r * 128 + 128)
        dual_out[:, part] = dual_ref[:, part] + sigma * (
            demand_ref[:, part] - result[r * 8 : r * 8 + 8]
        )


def to_other_core(x):
    return lax.ppermute(x, CORE, [(0, 1), (1, 0)])


def exchange(pieces, axis):
    return lax.all_to_all(pieces, axis, split_axis=0, concat_axis=0, tiled=True)


def in_hbm(x):
    return pltpu.with_memory_space_constraint(x, pltpu.HBM)


def on_device(
    blocks, column_index, block_period, cost_vector, demand, primal_start, dual_start, primal_weight
):
    partials = shaped(PEERS * PIECE, 128)
    pieces = (PEERS, PIECE, 128)
    chunk = shaped(CHUNK, 128)
    local = shaped(8, 256)
    pack = shaped(16, 128)
    rows = pltpu.VMEM((CHUNK, 128), f32)

    places = [pltpu.SMEM((96,), jnp.int32), pltpu.SemaphoreType.DMA(())]
    index, partial, kept = call(
        adjoint_start,
        [jax.ShapeDtypeStruct((96,), jnp.int32), partials, shaped(*blocks.shape)],
        [HBM] * 4,
        [
            pltpu.SMEM((6, 2, 8), jnp.int32),
            pltpu.SMEM((6, 2, 8), jnp.int32),
            places[0],
            pltpu.VMEM((8, 256), f32),
            pltpu.SemaphoreType.DMA((12,)),
        ],
    )(
        in_hbm(column_index.transpose(2, 1, 0)),
        in_hbm(block_period.transpose(2, 1, 0)),
        in_hbm(blocks),
        in_hbm(dual_start),
    )
    kept = pltpu.with_memory_space_constraint(kept, pltpu.VMEM)
    arrived = exchange(partial.reshape(pieces), PLANE)
    tiles = call(
        sum_first, shaped(LINE_PEERS, 56, 128), [VMEM] * 3, [pltpu.VMEM((56, 128), f32)]
    )(arrived, cost_vector, primal_start)
    tiles = exchange(tiles, LINE)
    other = to_other_core(call(for_other_core, pack, [VMEM])(tiles))
    send, primal_one, before_one, move_primal = call(
        primal_step,
        [shaped(*pieces), chunk, shaped(4, 128), shaped(1, 128)],
        [SMEM, VMEM, VMEM],
        [rows],
    )(primal_weight, tiles, other)
    field = exchange(send, PLANE).reshape(PEERS * PIECE, 128)
    dual_one, partial = call(
        dual_step, [local, partials], [VMEM, SMEM] + [VMEM] * 5, places
    )(
        index, primal_weight, kept, field, dual_start, demand, move_primal
    )
    arrived = exchange(partial.reshape(pieces), PLANE)
    tiles = call(sum_second, shaped(LINE_PEERS, PIECE, 128), [VMEM] * 2, [pltpu.VMEM((PIECE, 128), f32)])(
        arrived, cost_vector
    )
    tiles = exchange(tiles, LINE)
    other = to_other_core(call(for_other_core, pack, [VMEM])(tiles))
    send, primal, steps = call(
        primal_last, [shaped(*pieces), chunk, shaped(8, 128)], [SMEM] + [VMEM] * 4, [rows]
    )(primal_weight, tiles, other, primal_one, before_one)
    field = exchange(send, PLANE).reshape(PEERS * PIECE, 128)
    primal_final, dual_final = call(dual_last, [local, local], [VMEM] * 7, places)(
        index, kept, field, steps, dual_one, demand, primal
    )
    return primal_final, dual_final


def solution(mesh):
    finer = Mesh(mesh.devices.reshape(4, 2, 2, 2, 2, 2, 2), AXES)
    return jax.shard_map(
        on_device,
        mesh=finer,
        in_specs=(
            P(SECTION, DOM, None, None, None),
            P(SECTION, DOM, None),
            P(SECTION, DOM, None),
            P(SECTION, DOM),
            P(SECTION, DOM),
            P(SECTION, DOM),
            P(SECTION, DOM),
            P(),
        ),
        out_specs=(P(SECTION, DOM), P(SECTION, DOM)),
        check_vma=False,
    )
```

```python
import functools

import jax
import jax.numpy as jnp
from jax import lax
from jax.experimental import pallas as pl
from jax.experimental.pallas import tpu as pltpu
from jax.sharding import Mesh
from jax.sharding import PartitionSpec as P

AXES = ("section_0", "section_1", "dom_00", "dom_01", "dom_1", "dom_20", "dom_21")
SECTION = ("section_0", "section_1")
DOM = ("dom_00", "dom_01", "dom_1", "dom_20", "dom_21")
PLANE = ("dom_21", "dom_20", "dom_00", "dom_01")
TWIN = "dom_1"
LINE = ("section_0", "dom_1")
CORE = "section_1"

step_scale = 0.4
epsilon = 1e-06

PEERS = 16
LINE_PEERS = 8
PERIODS_HERE = 8
CHUNK = 32
PIECE = 40
HALO = slice(32, 36)

f32 = jnp.float32
VMEM = pl.BlockSpec(memory_space=pltpu.VMEM)
HBM = pl.BlockSpec(memory_space=pltpu.HBM)
SMEM = pl.BlockSpec(memory_space=pltpu.SMEM)
PARAMS = pltpu.CompilerParams(vmem_limit_bytes=32 << 20)


def shaped(*shape):
    return jax.ShapeDtypeStruct(shape, f32)


def call(kernel, outs, ins, scratch=()):
    return pl.pallas_call(
        kernel,
        out_shape=outs,
        in_specs=ins,
        out_specs=jax.tree.map(lambda _: VMEM, outs),
        scratch_shapes=list(scratch),
        compiler_params=PARAMS,
    )


def columns_of(ref):
    rows = jnp.concatenate([ref[:, :128], ref[:, 128:], jnp.zeros((112, 128), f32)], axis=0)
    return rows.T


def store_rows(ref, rows):
    ref[:, :128] = rows[0:8]
    ref[:, 128:] = rows[8:16]


def row_of(index_ref, t, r, k):
    return pl.ds(index_ref[t * 12 + r * 6 + k], 1)


def add_terms(blocks_ref, index_ref, dest_ref, t, r, wide):
    for k in range(6):
        term = jnp.sum(blocks_ref[t, r, k] * wide, axis=0, keepdims=True)
        dest_ref[row_of(index_ref, t, r, k), :] += term


def all_products(blocks_ref, index_ref, source_ref):
    lane = lax.broadcasted_iota(jnp.int32, (128, 128), 1)
    result = jnp.zeros((128, 128), f32)
    for t in range(PERIODS_HERE):
        for r in range(2):
            total = jnp.zeros((128, 128), f32)
            for k in range(6):
                total += blocks_ref[t, r, k] * source_ref[row_of(index_ref, t, r, k), :]
            product = jnp.sum(total, axis=1, keepdims=True)
            result = jnp.where(lane == r * 8 + t, jnp.broadcast_to(product, (128, 128)), result)
    return result


def wide_column(columns, t, r):
    place = r * 8 + t
    return jnp.broadcast_to(columns[:, place : place + 1], (128, 128))


def fill_index(column_ref, period_ref, index_ref, t):
    for r in range(2):
        for k in range(6):
            c = column_ref[k, r, t]
            before = lax.axis_index(SECTION) * PERIODS_HERE + t - period_ref[k, r, t]
            peer = ((c >> 1) & 1) * 8 + ((c >> 2) & 1) * 4 + ((c >> 5) & 1) * 2 + ((c >> 4) & 1) * 1
            inside = ((c >> 3) & 1) * 2 + (c & 1)
            row = inside * 8 + t - before
            if t == 0:
                row = jnp.where(before == 0, inside * 8, inside + CHUNK)
            index_ref[t * 12 + r * 6 + k] = peer * PIECE + row


def adjoint_start(
    column_in, period_in, blocks_in, dual_in, index_out, partial_ref, blocks_ref,
    column_ref, period_ref, index_ref, dual_ref, arrived,
):
    get_column = pltpu.make_async_copy(column_in, column_ref, arrived.at[0])
    get_period = pltpu.make_async_copy(period_in, period_ref, arrived.at[1])
    get_dual = pltpu.make_async_copy(dual_in, dual_ref, arrived.at[2])
    get_blocks = [
        pltpu.make_async_copy(blocks_in.at[t], blocks_ref.at[t], arrived.at[3 + t])
        for t in range(PERIODS_HERE)
    ]
    for copy in [get_column, get_period, get_dual] + get_blocks:
        copy.start()
    partial_ref[...] = jnp.zeros_like(partial_ref)
    get_dual.wait()
    columns = columns_of(dual_ref)
    get_column.wait()
    get_period.wait()
    for t in range(PERIODS_HERE):
        fill_index(column_ref, period_ref, index_ref, t)
    put_index = pltpu.make_async_copy(index_ref, index_out, arrived.at[11])
    put_index.start()
    for t in range(PERIODS_HERE):
        get_blocks[t].wait()
        for r in range(2):
            add_terms(blocks_ref, index_ref, partial_ref, t, r, wide_column(columns, t, r))
    put_index.wait()


def total_of(pieces_ref):
    total = pieces_ref[0]
    for p in range(1, PEERS):
        total = total + pieces_ref[p]
    return total


def to_all(ref, value, count):
    for p in range(count):
        ref[p] = value


def tile_of(tile, pieces_ref, cost_ref):
    tile[0:PIECE, :] = total_of(pieces_ref)
    own = pl.multiple_of(lax.axis_index(TWIN) * 16, 16)
    tile[pl.ds(own, 8), :] -= cost_ref[:, :128]
    tile[pl.ds(own + 8, 8), :] -= cost_ref[:, 128:]


def sum_first(pieces_ref, cost_ref, primal_ref, tiles_ref, tile):
    tile_of(tile, pieces_ref, cost_ref)
    tile[40:48, :] = primal_ref[:, :128]
    tile[48:56, :] = primal_ref[:, 128:]
    to_all(tiles_ref, tile[...], LINE_PEERS)


def sum_second(pieces_ref, cost_ref, tiles_ref, tile):
    tile_of(tile, pieces_ref, cost_ref)
    to_all(tiles_ref, tile[...], LINE_PEERS)


def for_other_core(tiles_ref, pack_ref):
    chip = lax.axis_index("section_0")
    core = lax.axis_index(CORE)
    above = 2 * jnp.minimum(chip + 1 - core, 3)
    below = 2 * jnp.maximum(chip - core, 0)
    pack_ref[...] = jnp.zeros_like(pack_ref)
    pack_ref[0:4, :] = tiles_ref[above, HALO] + tiles_ref[above + 1, HALO]
    for i in range(4):
        last = slice(8 * i + 7, 8 * i + 8)
        pack_ref[4 + i : 5 + i, :] = tiles_ref[below, last] + tiles_ref[below + 1, last]
    if tiles_ref.shape[1] > PIECE:
        for i in range(4):
            late = 47 + 8 * (i % 2)
            pack_ref[8 + i : 9 + i, :] = tiles_ref[below + i // 2, late : late + 1]
    moves = tiles_ref[0, 36:40]
    for d in range(1, LINE_PEERS):
        moves = moves + tiles_ref[d, 36:40]
    pack_ref[12:16, :] = moves


def descents(tiles_ref, other_ref, descent):
    section = lax.axis_index(SECTION)
    here = 2 * lax.axis_index("section_0")
    descent[...] = tiles_ref[here, 0:CHUNK] + tiles_ref[here + 1, 0:CHUNK]
    for i in range(4):
        carried = jnp.where(section < 7, other_ref[i : i + 1], 0.0)
        descent[8 * i + 7 : 8 * i + 8, :] += carried
    before = other_ref[4:8] + tiles_ref[here, HALO] + tiles_ref[here + 1, HALO]
    return descent[...], before


def send_field(copies_ref, field, before):
    to_all(copies_ref, jnp.concatenate([field, before, jnp.zeros((4, 128), f32)], 0), PEERS)


def primal_step(
    weight_ref, tiles_ref, other_ref, copies_ref, primal_one_ref, before_one_ref, move_ref, descent
):
    tau = step_scale / jnp.full((1, 128), weight_ref[0], f32)
    along, along_before = descents(tiles_ref, other_ref, descent)
    here = 2 * lax.axis_index("section_0")
    start = jnp.concatenate([tiles_ref[here, 40:56], tiles_ref[here + 1, 40:56]], 0)
    start_before = other_ref[8:12]
    primal_one = jnp.maximum(0.0, start + tau * along)
    before_one = jnp.maximum(0.0, start_before + tau * along_before)
    primal_one_ref[...] = primal_one
    before_one_ref[...] = before_one
    move_ref[...] = 0.5 * jnp.sum((primal_one - start) ** 2, axis=0, keepdims=True)
    send_field(copies_ref, 2.0 * primal_one - start, 2.0 * before_one - start_before)


def dual_step(
    index_in, weight_ref, blocks_ref, field_ref, dual_ref, demand_ref, move_x, dual_one_ref, partial_ref,
    index_ref, arrived,
):
    get_index = pltpu.make_async_copy(index_in, index_ref, arrived)
    get_index.start()
    partial_ref[...] = jnp.zeros_like(partial_ref)
    sigma = step_scale * weight_ref[0]
    start = columns_of(dual_ref)
    demand = columns_of(demand_ref)
    get_index.wait()
    product = all_products(blocks_ref, index_ref, field_ref)
    dual_one = start + sigma * (demand - product)
    for t in range(PERIODS_HERE):
        for r in range(2):
            add_terms(blocks_ref, index_ref, partial_ref, t, r, wide_column(dual_one, t, r))
    move = jnp.sum((dual_one - start).T ** 2, axis=0, keepdims=True)
    moves = jnp.concatenate([move_x[...], move], 0)
    for p in range(PEERS):
        partial_ref[p * PIECE + 36 : p * PIECE + 38, :] = moves
    store_rows(dual_one_ref, dual_one.T)


def primal_last(
    weight_ref, tiles_ref, other_ref, primal_one_ref, before_one_ref, copies_ref, primal_ref, steps_ref, descent
):
    moves = other_ref[8:16]
    for d in range(LINE_PEERS):
        moves = moves + tiles_ref[d, 32:40]
    move = jnp.broadcast_to(jnp.sum(moves, axis=1, keepdims=True), (8, 128))
    move_primal, move_dual = move[4:5], move[5:6]
    weight = jnp.full((1, 128), weight_ref[0], f32)
    omega = jnp.sqrt(weight * jnp.sqrt((move_dual + epsilon) / (move_primal + epsilon)))
    tau = step_scale / omega
    steps_ref[...] = jnp.broadcast_to(step_scale * omega, (8, 128))
    along, along_before = descents(tiles_ref, other_ref, descent)
    primal_one = primal_one_ref[...]
    before_one = before_one_ref[...]
    primal = jnp.maximum(0.0, primal_one + tau * along)
    before = jnp.maximum(0.0, before_one + tau * along_before)
    primal_ref[...] = primal
    send_field(copies_ref, 2.0 * primal - primal_one, 2.0 * before - before_one)


def dual_last(
    index_in, blocks_ref, field_ref, steps_ref, dual_ref, demand_ref, primal_ref, primal_out, dual_out,
    index_ref, arrived,
):
    get_index = pltpu.make_async_copy(index_in, index_ref, arrived)
    get_index.start()
    own = pl.multiple_of(lax.axis_index(TWIN) * 16, 16)
    primal_out[:, :128] = primal_ref[pl.ds(own, 8), :]
    primal_out[:, 128:] = primal_ref[pl.ds(own + 8, 8), :]
    get_index.wait()
    result = all_products(blocks_ref, index_ref, field_ref).T
    sigma = steps_ref[...]
    for r in range(2):
        part = slice(r * 128, r * 128 + 128)
        dual_out[:, part] = dual_ref[:, part] + sigma * (
            demand_ref[:, part] - result[r * 8 : r * 8 + 8]
        )


def to_other_core(x):
    return lax.ppermute(x, CORE, [(0, 1), (1, 0)])


def exchange(pieces, axis):
    return lax.all_to_all(pieces, axis, split_axis=0, concat_axis=0, tiled=True)


def in_hbm(x):
    return pltpu.with_memory_space_constraint(x, pltpu.HBM)


def on_device(
    blocks, column_index, block_period, cost_vector, demand, primal_start, dual_start, primal_weight
):
    partials = shaped(PEERS * PIECE, 128)
    pieces = (PEERS, PIECE, 128)
    chunk = shaped(CHUNK, 128)
    local = shaped(8, 256)
    pack = shaped(16, 128)
    rows = pltpu.VMEM((CHUNK, 128), f32)

    places = [pltpu.SMEM((96,), jnp.int32), pltpu.SemaphoreType.DMA(())]
    index, partial, kept = call(
        adjoint_start,
        [jax.ShapeDtypeStruct((96,), jnp.int32), partials, shaped(*blocks.shape)],
        [HBM] * 4,
        [
            pltpu.SMEM((6, 2, 8), jnp.int32),
            pltpu.SMEM((6, 2, 8), jnp.int32),
            places[0],
            pltpu.VMEM((8, 256), f32),
            pltpu.SemaphoreType.DMA((12,)),
        ],
    )(
        in_hbm(column_index.transpose(2, 1, 0)),
        in_hbm(block_period.transpose(2, 1, 0)),
        in_hbm(blocks),
        in_hbm(dual_start),
    )
    kept = pltpu.with_memory_space_constraint(kept, pltpu.VMEM)
    arrived = exchange(partial.reshape(pieces), PLANE)
    tiles = call(
        sum_first, shaped(LINE_PEERS, 56, 128), [VMEM] * 3, [pltpu.VMEM((56, 128), f32)]
    )(arrived, cost_vector, primal_start)
    tiles = exchange(tiles, LINE)
    other = to_other_core(call(for_other_core, pack, [VMEM])(tiles))
    send, primal_one, before_one, move_primal = call(
        primal_step,
        [shaped(*pieces), chunk, shaped(4, 128), shaped(1, 128)],
        [SMEM, VMEM, VMEM],
        [rows],
    )(primal_weight, tiles, other)
    field = exchange(send, PLANE).reshape(PEERS * PIECE, 128)
    dual_one, partial = call(
        dual_step, [local, partials], [VMEM, SMEM] + [VMEM] * 5, places
    )(
        index, primal_weight, kept, field, dual_start, demand, move_primal
    )
    arrived = exchange(partial.reshape(pieces), PLANE)
    tiles = call(sum_second, shaped(LINE_PEERS, PIECE, 128), [VMEM] * 2, [pltpu.VMEM((PIECE, 128), f32)])(
        arrived, cost_vector
    )
    tiles = exchange(tiles, LINE)
    other = to_other_core(call(for_other_core, pack, [VMEM])(tiles))
    send, primal, steps = call(
        primal_last, [shaped(*pieces), chunk, shaped(8, 128)], [SMEM] + [VMEM] * 4, [rows]
    )(primal_weight, tiles, other, primal_one, before_one)
    field = exchange(send, PLANE).reshape(PEERS * PIECE, 128)
    primal_final, dual_final = call(dual_last, [local, local], [VMEM] * 7, places)(
        index, kept, field, steps, dual_one, demand, primal
    )
    return primal_final, dual_final


def solution(mesh):
    finer = Mesh(mesh.devices.reshape(4, 2, 2, 2, 2, 2, 2), AXES)
    return jax.shard_map(
        on_device,
        mesh=finer,
        in_specs=(
            P(SECTION, DOM, None, None, None),
            P(SECTION, DOM, None),
            P(SECTION, DOM, None),
            P(SECTION, DOM),
            P(SECTION, DOM),
            P(SECTION, DOM),
            P(SECTION, DOM),
            P(),
        ),
        out_specs=(P(SECTION, DOM), P(SECTION, DOM)),
        check_vma=False,
    )
```

```python
import functools

import jax
import jax.numpy as jnp
from jax import lax
from jax.experimental import pallas as pl
from jax.experimental.pallas import tpu as pltpu
from jax.sharding import Mesh
from jax.sharding import PartitionSpec as P

AXES = ("section_00", "section_01", "section_1", "dom_00", "dom_01", "dom_1", "dom_20", "dom_21")
SECTION = ("section_00", "section_01", "section_1")
DOM = ("dom_00", "dom_01", "dom_1", "dom_20", "dom_21")
PLANE = ("dom_21", "dom_20", "dom_00", "dom_01")
TWIN = "dom_1"
LINE = ("section_01", "section_00", "dom_1")
CHIP = ("section_00", "section_01")
CORE = "section_1"

step_scale = 0.4
epsilon = 1e-06

PEERS = 16
LINE_PEERS = 8
PERIODS_HERE = 8
CHUNK = 32
PIECE = 40
HALO = slice(32, 36)

f32 = jnp.float32
VMEM = pl.BlockSpec(memory_space=pltpu.VMEM)
HBM = pl.BlockSpec(memory_space=pltpu.HBM)
SMEM = pl.BlockSpec(memory_space=pltpu.SMEM)
PARAMS = pltpu.CompilerParams(vmem_limit_bytes=32 << 20)


def shaped(*shape):
    return jax.ShapeDtypeStruct(shape, f32)


def call(kernel, outs, ins, scratch=()):
    return pl.pallas_call(
        kernel,
        out_shape=outs,
        in_specs=ins,
        out_specs=jax.tree.map(lambda _: VMEM, outs),
        scratch_shapes=list(scratch),
        compiler_params=PARAMS,
    )


def columns_of(ref):
    rows = jnp.concatenate([ref[:, :128], ref[:, 128:], jnp.zeros((112, 128), f32)], axis=0)
    return rows.T


def store_rows(ref, rows):
    ref[:, :128] = rows[0:8]
    ref[:, 128:] = rows[8:16]


def row_of(index_ref, t, r, k):
    return pl.ds(index_ref[t * 12 + r * 6 + k], 1)


def add_terms(blocks_ref, index_ref, dest_ref, t, r, wide):
    for k in range(6):
        term = jnp.sum(blocks_ref[t, r, k] * wide, axis=0, keepdims=True)
        dest_ref[row_of(index_ref, t, r, k), :] += term


def all_products(blocks_ref, index_ref, source_ref):
    lane = lax.broadcasted_iota(jnp.int32, (128, 128), 1)
    result = jnp.zeros((128, 128), f32)
    for t in range(PERIODS_HERE):
        for r in range(2):
            total = jnp.zeros((128, 128), f32)
            for k in range(6):
                total += blocks_ref[t, r, k] * source_ref[row_of(index_ref, t, r, k), :]
            product = jnp.sum(total, axis=1, keepdims=True)
            result = jnp.where(lane == r * 8 + t, jnp.broadcast_to(product, (128, 128)), result)
    return result


def wide_column(columns, t, r):
    place = r * 8 + t
    return jnp.broadcast_to(columns[:, place : place + 1], (128, 128))


def fill_index(column_ref, period_ref, index_ref, t):
    for r in range(2):
        for k in range(6):
            c = column_ref[k, r, t]
            before = lax.axis_index(SECTION) * PERIODS_HERE + t - period_ref[k, r, t]
            peer = ((c >> 1) & 1) * 8 + ((c >> 2) & 1) * 4 + ((c >> 5) & 1) * 2 + ((c >> 4) & 1) * 1
            inside = ((c >> 3) & 1) * 2 + (c & 1)
            row = inside * 8 + t - before
            if t == 0:
                row = jnp.where(before == 0, inside * 8, inside + CHUNK)
            index_ref[t * 12 + r * 6 + k] = peer * PIECE + row


def adjoint_start(
    column_in, period_in, blocks_in, dual_in, index_out, partial_ref, blocks_ref,
    column_ref, period_ref, index_ref, dual_ref, arrived,
):
    get_column = pltpu.make_async_copy(column_in, column_ref, arrived.at[0])
    get_period = pltpu.make_async_copy(period_in, period_ref, arrived.at[1])
    get_dual = pltpu.make_async_copy(dual_in, dual_ref, arrived.at[2])
    get_blocks = [
        pltpu.make_async_copy(blocks_in.at[t], blocks_ref.at[t], arrived.at[3 + t])
        for t in range(PERIODS_HERE)
    ]
    for copy in [get_column, get_period, get_dual] + get_blocks:
        copy.start()
    partial_ref[...] = jnp.zeros_like(partial_ref)
    get_dual.wait()
    columns = columns_of(dual_ref)
    get_column.wait()
    get_period.wait()
    for t in range(PERIODS_HERE):
        fill_index(column_ref, period_ref, index_ref, t)
    put_index = pltpu.make_async_copy(index_ref, index_out, arrived.at[11])
    put_index.start()
    for t in range(PERIODS_HERE):
        get_blocks[t].wait()
        for r in range(2):
            add_terms(blocks_ref, index_ref, partial_ref, t, r, wide_column(columns, t, r))
    put_index.wait()


def total_of(pieces_ref):
    total = pieces_ref[0]
    for p in range(1, PEERS):
        total = total + pieces_ref[p]
    return total


def to_all(ref, value, count):
    for p in range(count):
        ref[p] = value


def tile_of(tile, pieces_ref, cost_ref):
    tile[0:PIECE, :] = total_of(pieces_ref)
    own = pl.multiple_of(lax.axis_index(TWIN) * 16, 16)
    tile[pl.ds(own, 8), :] -= cost_ref[:, :128]
    tile[pl.ds(own + 8, 8), :] -= cost_ref[:, 128:]


def sum_first(pieces_ref, cost_ref, primal_ref, tiles_ref, tile):
    tile_of(tile, pieces_ref, cost_ref)
    tile[40:48, :] = primal_ref[:, :128]
    tile[48:56, :] = primal_ref[:, 128:]
    to_all(tiles_ref, tile[...], LINE_PEERS)


def sum_second(pieces_ref, cost_ref, tiles_ref, tile):
    tile_of(tile, pieces_ref, cost_ref)
    to_all(tiles_ref, tile[...], LINE_PEERS)


def tile_place(chip):
    return (chip & 1) * 4 + (chip >> 1) * 2


def for_other_core(tiles_ref, pack_ref):
    chip = lax.axis_index(CHIP)
    core = lax.axis_index(CORE)
    above = tile_place(jnp.minimum(chip + 1 - core, 3))
    below = tile_place(jnp.maximum(chip - core, 0))
    pack_ref[...] = jnp.zeros_like(pack_ref)
    pack_ref[0:4, :] = tiles_ref[above, HALO] + tiles_ref[above + 1, HALO]
    for i in range(4):
        last = slice(8 * i + 7, 8 * i + 8)
        pack_ref[4 + i : 5 + i, :] = tiles_ref[below, last] + tiles_ref[below + 1, last]
    if tiles_ref.shape[1] > PIECE:
        for i in range(4):
            late = 47 + 8 * (i % 2)
            pack_ref[8 + i : 9 + i, :] = tiles_ref[below + i // 2, late : late + 1]
    moves = tiles_ref[0, 36:40]
    for d in range(1, LINE_PEERS):
        moves = moves + tiles_ref[d, 36:40]
    pack_ref[12:16, :] = moves


def descents(tiles_ref, other_ref, descent):
    section = lax.axis_index(SECTION)
    here = tile_place(lax.axis_index(CHIP))
    descent[...] = tiles_ref[here, 0:CHUNK] + tiles_ref[here + 1, 0:CHUNK]
    for i in range(4):
        carried = jnp.where(section < 7, other_ref[i : i + 1], 0.0)
        descent[8 * i + 7 : 8 * i + 8, :] += carried
    before = other_ref[4:8] + tiles_ref[here, HALO] + tiles_ref[here + 1, HALO]
    return descent[...], before


def send_field(copies_ref, field, before):
    to_all(copies_ref, jnp.concatenate([field, before, jnp.zeros((4, 128), f32)], 0), PEERS)


def primal_step(
    weight_ref, tiles_ref, other_ref, copies_ref, primal_one_ref, before_one_ref, move_ref, descent
):
    tau = step_scale / jnp.full((1, 128), weight_ref[0], f32)
    along, along_before = descents(tiles_ref, other_ref, descent)
    here = tile_place(lax.axis_index(CHIP))
    start = jnp.concatenate([tiles_ref[here, 40:56], tiles_ref[here + 1, 40:56]], 0)
    start_before = other_ref[8:12]
    primal_one = jnp.maximum(0.0, start + tau * along)
    before_one = jnp.maximum(0.0, start_before + tau * along_before)
    primal_one_ref[...] = primal_one
    before_one_ref[...] = before_one
    move_ref[...] = 0.5 * jnp.sum((primal_one - start) ** 2, axis=0, keepdims=True)
    send_field(copies_ref, 2.0 * primal_one - start, 2.0 * before_one - start_before)


def dual_step(
    index_in, weight_ref, blocks_ref, field_ref, dual_ref, demand_ref, move_x, dual_one_ref, partial_ref,
    index_ref, arrived,
):
    get_index = pltpu.make_async_copy(index_in, index_ref, arrived)
    get_index.start()
    partial_ref[...] = jnp.zeros_like(partial_ref)
    sigma = step_scale * weight_ref[0]
    start = columns_of(dual_ref)
    demand = columns_of(demand_ref)
    get_index.wait()
    product = all_products(blocks_ref, index_ref, field_ref)
    dual_one = start + sigma * (demand - product)
    for t in range(PERIODS_HERE):
        for r in range(2):
            add_terms(blocks_ref, index_ref, partial_ref, t, r, wide_column(dual_one, t, r))
    move = jnp.sum((dual_one - start).T ** 2, axis=0, keepdims=True)
    moves = jnp.concatenate([move_x[...], move], 0)
    for p in range(PEERS):
        partial_ref[p * PIECE + 36 : p * PIECE + 38, :] = moves
    store_rows(dual_one_ref, dual_one.T)


def primal_last(
    weight_ref, tiles_ref, other_ref, primal_one_ref, before_one_ref, copies_ref, primal_ref, steps_ref, descent
):
    moves = other_ref[8:16]
    for d in range(LINE_PEERS):
        moves = moves + tiles_ref[d, 32:40]
    move = jnp.broadcast_to(jnp.sum(moves, axis=1, keepdims=True), (8, 128))
    move_primal, move_dual = move[4:5], move[5:6]
    weight = jnp.full((1, 128), weight_ref[0], f32)
    omega = jnp.sqrt(weight * jnp.sqrt((move_dual + epsilon) / (move_primal + epsilon)))
    tau = step_scale / omega
    steps_ref[...] = jnp.broadcast_to(step_scale * omega, (8, 128))
    along, along_before = descents(tiles_ref, other_ref, descent)
    primal_one = primal_one_ref[...]
    before_one = before_one_ref[...]
    primal = jnp.maximum(0.0, primal_one + tau * along)
    before = jnp.maximum(0.0, before_one + tau * along_before)
    primal_ref[...] = primal
    send_field(copies_ref, 2.0 * primal - primal_one, 2.0 * before - before_one)


def dual_last(
    index_in, blocks_ref, field_ref, steps_ref, dual_ref, demand_ref, primal_ref, primal_out, dual_out,
    index_ref, arrived,
):
    get_index = pltpu.make_async_copy(index_in, index_ref, arrived)
    get_index.start()
    own = pl.multiple_of(lax.axis_index(TWIN) * 16, 16)
    primal_out[:, :128] = primal_ref[pl.ds(own, 8), :]
    primal_out[:, 128:] = primal_ref[pl.ds(own + 8, 8), :]
    get_index.wait()
    result = all_products(blocks_ref, index_ref, field_ref).T
    sigma = steps_ref[...]
    for r in range(2):
        part = slice(r * 128, r * 128 + 128)
        dual_out[:, part] = dual_ref[:, part] + sigma * (
            demand_ref[:, part] - result[r * 8 : r * 8 + 8]
        )


def to_other_core(x):
    return lax.ppermute(x, CORE, [(0, 1), (1, 0)])


def exchange(pieces, axis):
    return lax.all_to_all(pieces, axis, split_axis=0, concat_axis=0, tiled=True)


def in_hbm(x):
    return pltpu.with_memory_space_constraint(x, pltpu.HBM)


def on_device(
    blocks, column_index, block_period, cost_vector, demand, primal_start, dual_start, primal_weight
):
    partials = shaped(PEERS * PIECE, 128)
    pieces = (PEERS, PIECE, 128)
    chunk = shaped(CHUNK, 128)
    local = shaped(8, 256)
    pack = shaped(16, 128)
    rows = pltpu.VMEM((CHUNK, 128), f32)

    places = [pltpu.SMEM((96,), jnp.int32), pltpu.SemaphoreType.DMA(())]
    index, partial, kept = call(
        adjoint_start,
        [jax.ShapeDtypeStruct((96,), jnp.int32), partials, shaped(*blocks.shape)],
        [HBM] * 4,
        [
            pltpu.SMEM((6, 2, 8), jnp.int32),
            pltpu.SMEM((6, 2, 8), jnp.int32),
            places[0],
            pltpu.VMEM((8, 256), f32),
            pltpu.SemaphoreType.DMA((12,)),
        ],
    )(
        in_hbm(column_index.transpose(2, 1, 0)),
        in_hbm(block_period.transpose(2, 1, 0)),
        in_hbm(blocks),
        in_hbm(dual_start),
    )
    kept = pltpu.with_memory_space_constraint(kept, pltpu.VMEM)
    arrived = exchange(partial.reshape(pieces), PLANE)
    tiles = call(
        sum_first, shaped(LINE_PEERS, 56, 128), [VMEM] * 3, [pltpu.VMEM((56, 128), f32)]
    )(arrived, cost_vector, primal_start)
    tiles = exchange(tiles, LINE)
    other = to_other_core(call(for_other_core, pack, [VMEM])(tiles))
    send, primal_one, before_one, move_primal = call(
        primal_step,
        [shaped(*pieces), chunk, shaped(4, 128), shaped(1, 128)],
        [SMEM, VMEM, VMEM],
        [rows],
    )(primal_weight, tiles, other)
    field = exchange(send, PLANE).reshape(PEERS * PIECE, 128)
    dual_one, partial = call(
        dual_step, [local, partials], [VMEM, SMEM] + [VMEM] * 5, places
    )(
        index, primal_weight, kept, field, dual_start, demand, move_primal
    )
    arrived = exchange(partial.reshape(pieces), PLANE)
    tiles = call(sum_second, shaped(LINE_PEERS, PIECE, 128), [VMEM] * 2, [pltpu.VMEM((PIECE, 128), f32)])(
        arrived, cost_vector
    )
    tiles = exchange(tiles, LINE)
    other = to_other_core(call(for_other_core, pack, [VMEM])(tiles))
    send, primal, steps = call(
        primal_last, [shaped(*pieces), chunk, shaped(8, 128)], [SMEM] + [VMEM] * 4, [rows]
    )(primal_weight, tiles, other, primal_one, before_one)
    field = exchange(send, PLANE).reshape(PEERS * PIECE, 128)
    primal_final, dual_final = call(dual_last, [local, local], [VMEM] * 7, places)(
        index, kept, field, steps, dual_one, demand, primal
    )
    return primal_final, dual_final


def solution(mesh):
    finer = Mesh(mesh.devices.reshape(2, 2, 2, 2, 2, 2, 2, 2), AXES)
    return jax.shard_map(
        on_device,
        mesh=finer,
        in_specs=(
            P(SECTION, DOM, None, None, None),
            P(SECTION, DOM, None),
            P(SECTION, DOM, None),
            P(SECTION, DOM),
            P(SECTION, DOM),
            P(SECTION, DOM),
            P(SECTION, DOM),
            P(),
        ),
        out_specs=(P(SECTION, DOM), P(SECTION, DOM)),
        check_vma=False,
    )
```
